32 devices in a mesh: doc: 8 (over z, y), leaf: 4 (over x, core).
Axes of the slice: x: 2, y: 2, z: 4, core: 2. Of those that a mesh axis runs over, the one named last changes fastest.
Arguments:
- features: bfloat16 [32768, 256], P(('doc', 'leaf'))
- scores: float32 [32768], P(('doc', 'leaf')), may hold values from -6 to 6
- labels: int32 [32768], P(('doc', 'leaf')), may hold values from 0 to 4
- query_ids: int32 [32768], P(('doc', 'leaf')), may hold values from 0 to 1018, as said below
- ranks: int32 [32768], P(('doc', 'leaf')), may hold values from 1 to 128, as said below
- leaf_ids: int32 [32768], P(('doc', 'leaf')), may hold values from 0 to 15
Outputs:
- gradients: float32 [32768], P(('doc', 'leaf'))
- tree_output: float32 [32768], P(('doc', 'leaf'))
- new_scores: float32 [32768], P(('doc', 'leaf'))
The draws below stay inside these ranges and needn't reach their ends.
Inputs may be any that keep to these rules, and one draw needn't show every extreme that they name: `query_ids`: the rows of one query are contiguous; ids are 0 on the first row and rise by one at each new query; a query has 1 to 128 rows and some query has exactly 128. Within each query the ranks of its rows are the numbers 1 to its row count, each once.
All inputs are finite; a program needn't handle non-finite values.
Results may differ from the reference program's by a relative error of at most 0.0038.
Values sent between devices are 32-bit elements; how exact they have to be, the bound alone decides.
No kernel may reach another device: no remote copies, remote signals or barrier semaphores. Data moves between devices by JAX's collectives and lax.ppermute only.
A program may use at most 64 MiB of HBM per device.

```python
import math
import jax
import jax.numpy as jnp
import numpy as np
from jax import lax

F = 256
LEAVES = 16
MAXQ = 128
ROWS_DEV = 1024
ROWS = 32768


def shared_rows(key):
    key_parts = jax.random.split(jax.random.fold_in(key, 7001), 6)
    frame_total = ROWS // MAXQ + 1
    frame_phase = jax.random.randint(key_parts[0], (), 1, MAXQ)
    full_frame = (jax.random.randint(key_parts[1], (), 1, ROWS // ROWS_DEV) * ROWS_DEV + frame_phase) // MAXQ
    cut_scores = jax.random.randint(key_parts[2], (frame_total, MAXQ - 1), 0, 1024) * MAXQ + jnp.arange(MAXQ - 1)[None, :]
    cut_points = (jnp.argsort(cut_scores, axis=1)[:, :3] + 1).astype(jnp.int32)
    frame_numbers = jnp.arange(frame_total)
    cut_count = jnp.where((frame_numbers == full_frame) | (frame_numbers == 0) | (frame_numbers == frame_total - 1), 0, 3)
    positions = jnp.arange(ROWS)
    shifted = positions + frame_phase
    frame_index = shifted // MAXQ
    frame_offset = shifted % MAXQ
    chosen = (cut_points[frame_index] == frame_offset[:, None]) & (jnp.arange(3)[None, :] < cut_count[frame_index][:, None])
    new_query = (frame_offset == 0) | (positions == 0) | jnp.any(chosen, axis=1)
    query_ids = (jnp.cumsum(new_query.astype(jnp.int32)) - 1).astype(jnp.int32)
    order_key = (jax.random.randint(key_parts[4], (ROWS,), 0, MAXQ) * MAXQ + frame_offset).astype(jnp.int32)
    frame_query = lax.dynamic_update_slice(jnp.full((frame_total * MAXQ,), -1, jnp.int32), query_ids, (frame_phase,)).reshape(frame_total, MAXQ)
    frame_key = lax.dynamic_update_slice(jnp.zeros((frame_total * MAXQ,), jnp.int32), order_key, (frame_phase,)).reshape(frame_total, MAXQ)
    earlier = (frame_query[:, None, :] == frame_query[:, :, None]) & (frame_key[:, None, :] < frame_key[:, :, None])
    frame_rank = 1 + jnp.sum(earlier.astype(jnp.int32), axis=2)
    rank_values = lax.dynamic_slice(frame_rank.reshape(-1), (frame_phase,), (ROWS,)).astype(jnp.int32)
    grade_draw = jax.random.randint(key_parts[5], (ROWS,), 0, 16)
    label_values = (grade_draw >= 8).astype(jnp.int32) + (grade_draw >= 12).astype(jnp.int32) + (grade_draw >= 14).astype(jnp.int32) + (grade_draw >= 15).astype(jnp.int32)
    return (query_ids, rank_values, label_values)


def draw_query_ids(key, part):
    return shared_rows(key)[0]


def draw_ranks(key, part):
    return shared_rows(key)[1]


def draw_labels(key, part):
    return shared_rows(key)[2]


def draw_features(key, part):
    label_values = shared_rows(key)[2].astype(jnp.float32)
    key_parts = jax.random.split(jax.random.fold_in(key, 7002), 4)
    common = jax.random.normal(key_parts[1], (ROWS,), jnp.float32)
    shared_dir = jax.random.normal(key_parts[2], (F,), jnp.float32)
    label_dir = 0.5 * jax.random.normal(key_parts[3], (F,), jnp.float32)
    noise = jax.random.normal(key_parts[0], (ROWS, F), jnp.float32)
    common_scale = 0.5
    values = noise + common_scale * common[:, None] * shared_dir[None, :] + 0.5 * (label_values - 1.0)[:, None] * label_dir[None, :]
    return values.astype(jnp.bfloat16)


def with_ends(values, own_key, least, largest):
    index_at = [jax.random.randint(jax.random.fold_in(own_key, axis), (), 0, length) for axis, length in enumerate(values.shape)]
    widest = values.shape.index(max(values.shape))
    beside = index_at[:widest] + [(index_at[widest] + 1) % values.shape[widest]] + index_at[widest + 1:]
    return values.at[tuple(index_at)].set(least).at[tuple(beside)].set(largest)


def block_scale(stream_key, dims, cuts, low, top_value):
    def one(dim, shards_of):
        steps = jax.random.uniform(jax.random.fold_in(jax.random.fold_in(stream_key, 6), dim), (shards_of,), jnp.float32, low / len(cuts), top_value / len(cuts))
        return jnp.repeat(jnp.exp(steps), dims[dim] // shards_of).reshape((-1,) + (1,) * (len(dims) - dim - 1))

    factor_of = one(*cuts[0])
    for cut in cuts[1:]:
        factor_of = factor_of * one(*cut)
    return factor_of


def cumulative_ranks(count, skew):
    weights = [(1 << 20) // math.isqrt(grade ** skew) + 1 for grade in range(1, count + 1)]
    deviation = 1 + sum(weights) // (1 << 30)
    return np.cumsum(np.array([max(1, weight // deviation) for weight in weights]))


def ranked_ids(key, shape, count, slope):
    table = cumulative_ranks(count, slope)
    lot = jax.random.randint(jax.random.fold_in(key, 1), shape, 0, int(table[count - 1]))
    grade = jnp.searchsorted(jnp.asarray(table, jnp.int32), lot, side="right")
    return jax.random.permutation(jax.random.fold_in(key, 2), count)[grade].astype(jnp.int32)


def centred(stream_key, dims, spread, reach, shards=(), kind=jnp.bfloat16):
    factor_of = block_scale(stream_key, dims, shards, -0.22, 0.18) if shards else 1.0
    entries = jax.random.normal(stream_key, dims, jnp.float32) * spread * factor_of
    return jnp.minimum(jnp.maximum(entries, -reach), reach).astype(kind)


def setup_inputs(seed: int = 0) -> dict:
    arg_keys = jax.random.split(jax.random.key(seed), 7)
    features = draw_features(jax.random.fold_in(arg_keys[6], 71), 0)
    scores = centred(arg_keys[1], (ROWS,), 1.0, 6.0, ((0, 32),), jnp.float32)
    labels = draw_labels(jax.random.fold_in(arg_keys[6], 71), 0)
    query_ids = draw_query_ids(jax.random.fold_in(arg_keys[6], 71), 0)
    ranks = draw_ranks(jax.random.fold_in(arg_keys[6], 71), 0)
    leaf_ids = with_ends(ranked_ids(arg_keys[5], (ROWS,), LEAVES, 2), jax.random.fold_in(arg_keys[5], 3), 0, LEAVES - 1).astype(jnp.int32)
    return {"features": features, "scores": scores, "labels": labels, "query_ids": query_ids, "ranks": ranks, "leaf_ids": leaf_ids}


LAMBDA = 1.0
SHRINKAGE = 0.1

def discount(rank_values):
    return 1.0 / jnp.log2(1.0 + jnp.maximum(rank_values, 1.0))

def pair_block(own_rows, window):
    same_query = own_rows[0][:, None] == window[0][None, :]
    own_label = own_rows[1][:, None]
    far_label = window[1][None, :]
    counts = jnp.stack([jnp.sum(jnp.where(same_query & (far_label >= grade_level), 1.0, 0.0), axis=1) for grade_level in (1.0, 2.0, 3.0, 4.0)], axis=1)
    positions = jnp.arange(1, MAXQ + 1).astype(jnp.float32)
    prefix = jnp.sum(jnp.where(positions[None, None, :] <= counts[:, :, None], discount(positions)[None, None, :], 0.0), axis=2)
    ideal_gain = jnp.sum(prefix * jnp.array([1.0, 2.0, 4.0, 8.0], jnp.float32)[None, :], axis=1)
    inverse = 1.0 / jnp.maximum(ideal_gain, 1.0)
    gain_gap = jnp.abs(jnp.exp2(own_label) - jnp.exp2(far_label))
    disc_gap = jnp.abs(discount(own_rows[2])[:, None] - discount(window[2])[None, :])
    direction = jnp.sign(own_label - far_label)
    weight = jnp.where(same_query, gain_gap * disc_gap, 0.0)
    pair_prob = jax.nn.sigmoid(-direction * (own_rows[3][:, None] - window[3][None, :]))
    gradient = -inverse * jnp.sum(direction * weight * pair_prob, axis=1)
    hessian = inverse * jnp.sum(weight * pair_prob * (1.0 - pair_prob), axis=1)
    return (gradient, hessian)

def lambdas(padded, row_count):
    block_rows = min(512, row_count)
    zero_index = jnp.zeros((), jnp.int32)

    def one_block(block_start):
        own_rows = lax.dynamic_slice(padded, (zero_index, block_start + MAXQ), (4, block_rows))
        window = lax.dynamic_slice(padded, (zero_index, block_start), (4, block_rows + 2 * MAXQ))
        return pair_block(own_rows, window)
    starts = (jnp.arange(row_count // block_rows) * block_rows).astype(jnp.int32)
    gradients, hessians = lax.map(one_block, starts)
    return (gradients.reshape(-1), hessians.reshape(-1))

def solve_leaf(leaf_block):
    feature_count = leaf_block.shape[1]
    gram_matrix = leaf_block[:feature_count]
    weighted_sum = leaf_block[feature_count]
    moment = leaf_block[feature_count + 1]
    hess_total = leaf_block[feature_count + 2, 0]
    grad_total = leaf_block[feature_count + 2, 1]
    denominator = hess_total + LAMBDA
    system = gram_matrix + LAMBDA * jnp.eye(feature_count, dtype=jnp.float32) - weighted_sum[:, None] * weighted_sum[None, :] / denominator
    right_side = weighted_sum * grad_total / denominator - moment
    factor = jnp.linalg.cholesky(system)
    middle = lax.linalg.triangular_solve(factor, right_side[:, None], left_side=True, lower=True)
    coefficients = lax.linalg.triangular_solve(factor, middle, left_side=True, lower=True, transpose_a=True)[:, 0]
    intercept = -(grad_total + jnp.sum(weighted_sum * coefficients)) / denominator
    return (coefficients, intercept)

def reference(features, scores, labels, query_ids, ranks, leaf_ids):
    row_info = jnp.stack([(query_ids + 1).astype(jnp.float32), labels.astype(jnp.float32), ranks.astype(jnp.float32), scores])
    padded = jnp.pad(row_info, ((0, 0), (MAXQ, MAXQ)))
    gradients, hessians = lambdas(padded, row_info.shape[1])

    def leaf_terms(leaf_number):
        in_leaf = (leaf_ids == leaf_number).astype(jnp.float32)
        weighted = ((hessians * in_leaf)[:, None] * features).astype(jnp.bfloat16)
        gram_matrix = lax.dot_general(weighted.astype(jnp.float32), features.astype(jnp.float32), (((0,), (0,)), ((), ())), preferred_element_type=jnp.float32)
        weighted_sum = jnp.sum(weighted.astype(jnp.float32), axis=0)
        grad_low = (gradients * in_leaf).astype(jnp.bfloat16)
        moment = jnp.dot(grad_low.astype(jnp.float32), features.astype(jnp.float32), preferred_element_type=jnp.float32)
        total_rows = jnp.zeros((6, F), jnp.float32)
        total_rows = total_rows.at[0, 0].set(jnp.sum(hessians * in_leaf)).at[0, 1].set(jnp.sum(gradients * in_leaf))
        return jnp.concatenate([gram_matrix, weighted_sum[None, :], moment[None, :], total_rows], axis=0)
    all_terms = lax.map(leaf_terms, jnp.arange(LEAVES).astype(jnp.int32))
    coefficients, intercepts = jax.vmap(solve_leaf)(all_terms)
    per_leaf = jnp.dot(features.astype(jnp.float32), coefficients.T, precision=lax.Precision.HIGHEST) + intercepts[None, :]
    chosen = leaf_ids[:, None] == jnp.arange(LEAVES).astype(jnp.int32)[None, :]
    tree_output = jnp.sum(jnp.where(chosen, per_leaf, 0.0), axis=1)
    new_scores = scores + SHRINKAGE * tree_output
    return (gradients, tree_output, new_scores)
```

```python
import jax
import jax.numpy as jnp
import numpy as np
from jax import lax
from jax.experimental import pallas as pl
from jax.experimental.pallas import tpu as pltpu
from jax.sharding import PartitionSpec as P

LEAVES = 16
MAXQ = 128
LAMBDA = 1.0
SHRINKAGE = 0.1
AXES = ("doc", "leaf")
LANE = 128
EXTRA = 8
VMEM_LIMIT = 48 * 1024 * 1024
F32 = jnp.float32
BF16 = jnp.bfloat16


def iota(shape, dim):
    return lax.broadcasted_iota(jnp.int32, shape, dim)


def lanes_of(block_rows):
    return jnp.concatenate(
        [block_rows[b : b + 1, :] for b in range(block_rows.shape[0])], axis=1
    )


def pair_gram_kernel(
    where_ref, x_ref, score_ref, label_ref, query_ref, rank_ref, leaf_ref, before_ref, after_ref,
    grad_ref, keep_ref, send_ref,
    rows, cols, packed_cols, hess_rows, weighted, moment_s, hsum_s, total_s,
):
    blocks = score_ref.shape[0]
    n_rows, feats = x_ref.shape
    half = feats // 2
    core = where_ref[0]
    first = where_ref[1]
    last = where_ref[2]

    def with_halo(mid, slot):
        before = before_ref[slot : slot + 1, :]
        after = after_ref[slot : slot + 1, :]
        return jnp.concatenate([before, mid, after], axis=0)

    query = with_halo(query_ref[...].astype(F32), 0)
    block_at = iota(query.shape, 0)
    outside = ((block_at == 0) & (first == 1)) | ((block_at == blocks + 1) & (last == 1))
    query = jnp.where(outside, -1.0, query)
    label = with_halo(label_ref[...].astype(F32), 1)
    rank = with_halo(rank_ref[...].astype(F32), 2)
    score = with_halo(score_ref[...], 3)
    gain = jnp.exp2(label)
    disc = 1.0 / jnp.log2(1.0 + jnp.maximum(rank, 1.0))
    expo = jnp.exp(score)
    for slot, value in enumerate((query, gain, disc, expo)):
        rows[slot, 0 : blocks + 2, :] = value
        turned = value.T
        for b in range(blocks + 2):
            cols[slot, b * LANE : (b + 1) * LANE, :] = jnp.broadcast_to(
                turned[:, b : b + 1], (LANE, LANE)
            )
    grade = label.T
    turned = (
        jnp.where(grade >= 1.0, 1, 0)
        + jnp.where(grade >= 2.0, 1 << 8, 0)
        + jnp.where(grade >= 3.0, 1 << 16, 0)
        + jnp.where(grade >= 4.0, 1 << 24, 0)
    )
    for b in range(blocks + 2):
        packed_cols[b * LANE : (b + 1) * LANE, :] = jnp.broadcast_to(
            turned[:, b : b + 1], (LANE, LANE)
        )

    positions = iota((LANE, LANE), 0).astype(F32) + 1.0
    position_disc = 1.0 / jnp.log2(1.0 + positions)

    def one_block(b, carry):
        own_q = rows[0, pl.ds(b + 1, 1), :]
        own_g = rows[1, pl.ds(b + 1, 1), :]
        own_d = rows[2, pl.ds(b + 1, 1), :]
        own_e = rows[3, pl.ds(b + 1, 1), :]
        grad_sum = jnp.zeros((8, LANE), F32)
        hess_sum = jnp.zeros((8, LANE), F32)
        counts = jnp.zeros((8, LANE), jnp.int32)
        for chunk in range(3 * LANE // 8):
            at = pl.ds(pl.multiple_of(b * LANE + chunk * 8, 8), 8)
            far_e = cols[3, at, :]
            same = cols[0, at, :] == own_q
            gap = own_g - cols[1, at, :]
            signed = jnp.where(same, gap * jnp.abs(own_d - cols[2, at, :]), 0.0)
            inv = 1.0 / (own_e + far_e)
            scaled = signed * inv
            grad_sum = grad_sum + scaled * jnp.where(gap > 0.0, far_e, own_e)
            hess_sum = hess_sum + jnp.abs(scaled) * (far_e * inv)
            counts = counts + jnp.where(same, packed_cols[at, :], 0)
        count = jnp.sum(counts, axis=0, keepdims=True)
        grad = jnp.sum(grad_sum, axis=0, keepdims=True)
        hess = jnp.sum(hess_sum, axis=0, keepdims=True) * own_e
        ideal = jnp.zeros((LANE, LANE), F32)
        for k in range(4):
            count_k = (lax.shift_right_logical(count, 8 * k) & 255).astype(F32)
            ideal = ideal + jnp.where(positions <= count_k, float(1 << k), 0.0)
        ideal = jnp.sum(ideal * position_disc, axis=0, keepdims=True)
        norm = 1.0 / jnp.maximum(ideal, 1.0)
        grad_ref[pl.ds(b, 1), :] = -norm * grad
        hess_rows[pl.ds(b, 1), :] = norm * hess
        return carry

    lax.fori_loop(0, blocks, one_block, 0)

    hess_all = lanes_of(hess_rows[...])
    grad_all = lanes_of(grad_ref[...])
    leaf_all = lanes_of(leaf_ref[...])
    weighted[...] = (x_ref[...].astype(F32).T * hess_all).astype(BF16)
    member = leaf_all == iota((LEAVES, n_rows), 0)
    member_low = jnp.where(member, 1.0, 0.0).astype(BF16)
    grad_low = jnp.where(member, grad_all, 0.0).astype(BF16)
    moment_s[...] = jnp.dot(grad_low, x_ref[...], preferred_element_type=F32)
    hsum_s[...] = lax.dot_general(
        member_low, weighted[...], (((1,), (1,)), ((), ())), preferred_element_type=F32
    )
    htot = jnp.sum(jnp.where(member, hess_all, 0.0), axis=1, keepdims=True)
    gtot = jnp.sum(jnp.where(member, grad_all, 0.0), axis=1, keepdims=True)
    lane_at = iota((LEAVES, LANE), 1)
    total_s[...] = jnp.where(lane_at == 0, htot, jnp.where(lane_at == 1, gtot, 0.0))

    down = iota((half, half), 0)
    across = iota((half, half), 1)

    def one_leaf(leaf, carry):
        mask = jnp.where(leaf_all == leaf, 1.0, 0.0).astype(BF16)
        gram = jnp.dot(weighted[...] * mask, x_ref[...], preferred_element_type=F32)
        corner = gram[half:, :half]
        mixed = jnp.where(down >= across, gram[:half, :half], gram[half:, half:])
        diagonal = jnp.sum(
            jnp.where(down == across, gram[half:, half:], 0.0), axis=0, keepdims=True
        )
        hs = hsum_s[pl.ds(leaf, 1), :]
        mo = moment_s[pl.ds(leaf, 1), :]
        to = total_s[pl.ds(leaf, 1), :]
        rest = jnp.zeros((EXTRA - 4, LANE), F32)
        extra0 = jnp.concatenate([diagonal, hs[:, :half], hs[:, half:], to, rest], axis=0)
        rest = jnp.zeros((EXTRA - 2, LANE), F32)
        extra1 = jnp.concatenate([mo[:, :half], mo[:, half:], rest], axis=0)
        keep_ref[leaf, :half, :] = jnp.where(core == 0, corner, mixed)
        send_ref[leaf, :half, :] = jnp.where(core == 0, mixed, corner)
        keep_ref[leaf, half:, :] = jnp.where(core == 0, extra0, extra1)
        send_ref[leaf, half:, :] = jnp.where(core == 0, extra1, extra0)
        return carry

    lax.fori_loop(0, LEAVES, one_leaf, 0)


def pair_gram(where, x, score, label, query, rank, leaf, before, after):
    blocks = score.shape[0]
    n_rows, feats = x.shape
    vmem = pl.BlockSpec(memory_space=pltpu.VMEM)
    high = feats // 2 + EXTRA
    part = jax.ShapeDtypeStruct((LEAVES, high, LANE), F32)
    return pl.pallas_call(
        pair_gram_kernel,
        out_shape=(jax.ShapeDtypeStruct((blocks, LANE), F32), part, part),
        in_specs=[pl.BlockSpec(memory_space=pltpu.SMEM)] + [vmem] * 8,
        out_specs=(vmem, vmem, vmem),
        scratch_shapes=[
            pltpu.VMEM((4, blocks + 8, LANE), F32),
            pltpu.VMEM((4, (blocks + 2) * LANE, LANE), F32),
            pltpu.VMEM(((blocks + 2) * LANE, LANE), jnp.int32),
            pltpu.VMEM((blocks, LANE), F32),
            pltpu.VMEM((feats, n_rows), BF16),
            pltpu.VMEM((LEAVES, feats), F32),
            pltpu.VMEM((LEAVES, feats), F32),
            pltpu.VMEM((LEAVES, LANE), F32),
        ],
        compiler_params=pltpu.CompilerParams(vmem_limit_bytes=VMEM_LIMIT),
    )(where, x, score, label, query, rank, leaf, before, after)


def block_inverse(block):
    size = block.shape[0]
    down = iota((size, size), 0)
    across = iota((size, size), 1)
    for p in range(size):
        column = jnp.broadcast_to(block[:, p : p + 1], (size, size))
        pivot = column[p : p + 1, :]
        row = jnp.where(across[:1, :] == p, 1.0, block[p : p + 1, :]) / pivot
        column = jnp.where(down == p, -1.0, column)
        rest = jnp.where((down == p) | (across == p), 0.0, block)
        block = rest - column * row
    return block


def exact_dot(a, b):
    return jnp.dot(a, b, precision=lax.Precision.HIGHEST, preferred_element_type=F32)


def solve_kernel(where_ref, own_ref, other_ref, out_ref, work):
    core = where_ref[0]
    high = own_ref.shape[0]
    half = high - EXTRA
    feats = 2 * half
    copies = out_ref.shape[0]
    block = 32
    own = own_ref[...]
    other = other_ref[...]
    part0 = jnp.where(core == 0, own, other)
    part1 = jnp.where(core == 0, other, own)
    corner = part0[:half]
    mixed = part1[:half]
    turned = mixed.T
    down = iota((half, half), 0)
    across = iota((half, half), 1)
    diag_row = part0[half : half + 1]
    upper_left = jnp.where(down >= across, mixed, turned)
    lower_right = jnp.where(down < across, mixed, jnp.where(down > across, turned, diag_row))
    hs0 = part0[half + 1 : half + 2]
    hs1 = part0[half + 2 : half + 3]
    htot = part0[half + 3 : half + 4, 0:1]
    gtot = part0[half + 3 : half + 4, 1:2]
    inv_den = 1.0 / (htot + LAMBDA)
    rhs0 = hs0 * (gtot * inv_den) - part1[half : half + 1]
    rhs1 = hs1 * (gtot * inv_den) - part1[half + 1 : half + 2]
    columns = jnp.concatenate(
        [hs0, hs1, rhs0, rhs1, jnp.zeros((4, LANE), F32)], axis=0
    ).T
    hc0 = columns[:, 0:1] * inv_den
    hc1 = columns[:, 1:2] * inv_den
    eye = jnp.where(down == across, LAMBDA, 0.0)
    work[0:half, 0:half] = upper_left + eye - hc0 * hs0
    work[0:half, half:feats] = corner.T - hc0 * hs1
    work[half:feats, 0:half] = corner - hc1 * hs0
    work[half:feats, half:feats] = lower_right + eye - hc1 * hs1
    work[0:half, feats:] = jnp.where(across == 0, columns[:, 2:3], 0.0)
    work[half:feats, feats:] = jnp.where(across == 0, columns[:, 3:4], 0.0)

    for start in range(0, feats, block):
        stop = start + block
        tile = (start // LANE) * LANE
        inverse = block_inverse(work[start:stop, start:stop])
        scaled = exact_dot(inverse, work[start:stop, tile:])
        if start > 0:
            work[0:start, tile:] = work[0:start, tile:] - exact_dot(
                work[0:start, start:stop], scaled
            )
        if stop < feats:
            work[stop:feats, tile:] = work[stop:feats, tile:] - exact_dot(
                work[stop:feats, start:stop], scaled
            )
        work[start:stop, tile:] = scaled

    w0 = work[0:half, feats:].T[0:1, :]
    w1 = work[half:feats, feats:].T[0:1, :]
    dotted = jnp.sum(hs0 * w0 + hs1 * w1, axis=1, keepdims=True)
    intercept = -(gtot + dotted) * inv_den
    result = jnp.concatenate(
        [w0, w1, jnp.broadcast_to(intercept, (1, LANE)), jnp.zeros((1, LANE), F32)], axis=0
    )
    out_ref[...] = jnp.broadcast_to(result[None], (copies, 4, LANE))


def solve_leaf(where, own, other, copies):
    high = own.shape[0]
    feats = 2 * (high - EXTRA)
    vmem = pl.BlockSpec(memory_space=pltpu.VMEM)
    return pl.pallas_call(
        solve_kernel,
        out_shape=jax.ShapeDtypeStruct((copies, 4, LANE), F32),
        in_specs=[pl.BlockSpec(memory_space=pltpu.SMEM), vmem, vmem],
        out_specs=vmem,
        scratch_shapes=[pltpu.VMEM((feats, feats + LANE), F32)],
        compiler_params=pltpu.CompilerParams(vmem_limit_bytes=VMEM_LIMIT),
    )(where, own, other)


def output_kernel(owners, x_ref, coef_ref, score_ref, leaf_ref, tree_ref, new_ref):
    low = jnp.concatenate([coef_ref[d, 0:1, :] for d in owners], axis=0)
    high = jnp.concatenate([coef_ref[d, 1:2, :] for d in owners], axis=0)
    shift = jnp.concatenate([coef_ref[d, 2:3, :] for d in owners], axis=0)[:, 0:1]
    coefs = jnp.concatenate([low, high], axis=1)
    top = coefs.astype(BF16)
    left = coefs - top.astype(F32)
    middle = left.astype(BF16)
    bottom = (left - middle.astype(F32)).astype(BF16)
    stacked = jnp.concatenate([top, middle, bottom], axis=0)
    parts = lax.dot_general(
        stacked, x_ref[...], (((1,), (1,)), ((), ())), preferred_element_type=F32
    )
    per_leaf = (
        parts[:LEAVES] + (parts[LEAVES : 2 * LEAVES] + parts[2 * LEAVES :])
    ) + shift
    leaf_all = lanes_of(leaf_ref[...])
    chosen = jnp.sum(
        jnp.where(leaf_all == iota(per_leaf.shape, 0), per_leaf, 0.0), axis=0, keepdims=True
    )
    for b in range(score_ref.shape[0]):
        piece = chosen[:, b * LANE : (b + 1) * LANE]
        tree_ref[b : b + 1, :] = piece
        new_ref[b : b + 1, :] = score_ref[b : b + 1, :] + SHRINKAGE * piece


def row_outputs(owners, x, coefs, score, leaf):
    vmem = pl.BlockSpec(memory_space=pltpu.VMEM)
    shape = jax.ShapeDtypeStruct(score.shape, F32)
    return pl.pallas_call(
        lambda *refs: output_kernel(owners, *refs),
        out_shape=(shape, shape),
        in_specs=[vmem] * 4,
        out_specs=(vmem, vmem),
        compiler_params=pltpu.CompilerParams(vmem_limit_bytes=VMEM_LIMIT),
    )(x, coefs, score, leaf)


def split_plan(docs, leaf_devices):
    cores = 2
    spread = leaf_devices // cores
    low_docs = 2 if docs % 2 == 0 else 1
    high_docs = docs // low_docs

    def device(high, low, across, core):
        return (high * low_docs + low) * leaf_devices + across * cores + core

    near = [
        [device(h, l, a, c) for l in range(low_docs) for a in range(spread)]
        for h in range(high_docs)
        for c in range(cores)
    ]
    far = [
        [device(h, l, a, c) for h in range(high_docs)]
        for l in range(low_docs)
        for a in range(spread)
        for c in range(cores)
    ]
    return near, far


def reduce_groups(parts, groups, leaf_of):
    size = len(groups[0])
    held = parts.shape[0]
    if held % size == 0:
        own = held // size
        arrived = lax.all_to_all(parts, AXES, 0, 0, axis_index_groups=groups, tiled=True)
        total = jnp.sum(arrived.reshape((size, own) + parts.shape[1:]), axis=0)
        for group in groups:
            for place, device in enumerate(group):
                leaf_of[device] = leaf_of[device][place * own : (place + 1) * own]
        return total
    return lax.psum(parts, AXES, axis_index_groups=groups)


def body(features, scores, labels, query_ids, ranks, leaf_ids):
    docs = lax.axis_size("doc")
    leaf_devices = lax.axis_size("leaf")
    devices = docs * leaf_devices
    n_rows = features.shape[0]
    me = lax.axis_index(AXES)
    where = jnp.stack(
        [me % 2, (me == 0).astype(jnp.int32), (me == devices - 1).astype(jnp.int32)]
    ).astype(jnp.int32)
    blocked = [
        v.reshape(n_rows // LANE, LANE) for v in (scores, labels, query_ids, ranks, leaf_ids)
    ]
    score, label, query, rank, leaf = blocked

    def edge(block):
        return jnp.stack(
            [
                query[block].astype(F32),
                label[block].astype(F32),
                rank[block].astype(F32),
                score[block],
            ]
        )

    ahead = [(i, i + 1) for i in range(devices - 1)]
    behind = [(i + 1, i) for i in range(devices - 1)]
    before = lax.ppermute(edge(n_rows // LANE - 1), AXES, ahead)
    after = lax.ppermute(edge(0), AXES, behind)

    grad, keep, send = pair_gram(
        where, features, score, label, query, rank, leaf, before, after
    )
    swap = [(i, i ^ 1) for i in range(devices)]
    mine = keep + lax.ppermute(send, AXES, swap)

    near, far = split_plan(docs, leaf_devices)
    leaf_of = [list(range(LEAVES)) for _ in range(devices)]
    mine = reduce_groups(mine, near, leaf_of)
    mine = reduce_groups(mine, far, leaf_of)
    mine = mine[0]
    other = lax.ppermute(mine, AXES, swap)
    coefs = solve_leaf(where, mine, other, devices)
    coefs = lax.all_to_all(coefs, AXES, 0, 0, tiled=True)
    owners = [leaf_of.index([l]) for l in range(LEAVES)]
    tree, fresh = row_outputs(owners, features, coefs, score, leaf)
    return grad.reshape(-1), tree.reshape(-1), fresh.reshape(-1)


def solution(mesh):
    rows = P(AXES)
    return jax.shard_map(
        body,
        mesh=mesh,
        in_specs=(P(AXES, None), rows, rows, rows, rows, rows),
        out_specs=(rows, rows, rows),
        check_vma=False,
    )
```

```python
import jax
import jax.numpy as jnp
import numpy as np
from jax import lax
from jax.experimental import pallas as pl
from jax.experimental.pallas import tpu as pltpu
from jax.sharding import PartitionSpec as P

LEAVES = 16
MAXQ = 128
LAMBDA = 1.0
SHRINKAGE = 0.1
AXES = ("doc", "leaf")
LANE = 128
EXTRA = 8
STRIP = 32
GROUP = 16
VMEM_LIMIT = 48 * 1024 * 1024
F32 = jnp.float32
BF16 = jnp.bfloat16


def iota(shape, dim):
    return lax.broadcasted_iota(jnp.int32, shape, dim)


def lanes_of(block_rows):
    return jnp.concatenate(
        [block_rows[b : b + 1, :] for b in range(block_rows.shape[0])], axis=1
    )


def pair_gram_kernel(
    where_ref, x_ref, score_ref, label_ref, query_ref, rank_ref, leaf_ref, before_ref, after_ref,
    grad_ref, keep_ref, send_ref,
    rows, cols, packed_cols, hess_rows, weighted, moment_s, hsum_s, total_s,
):
    blocks = score_ref.shape[0]
    n_rows, feats = x_ref.shape
    half = feats // 2
    core = where_ref[0]
    first = where_ref[1]
    last = where_ref[2]

    def with_halo(mid, slot):
        before = before_ref[slot : slot + 1, :]
        after = after_ref[slot : slot + 1, :]
        return jnp.concatenate([before, mid, after], axis=0)

    query = with_halo(query_ref[...].astype(F32), 0)
    block_at = iota(query.shape, 0)
    outside = ((block_at == 0) & (first == 1)) | ((block_at == blocks + 1) & (last == 1))
    query = jnp.where(outside, -1.0, query)
    label = with_halo(label_ref[...].astype(F32), 1)
    rank = with_halo(rank_ref[...].astype(F32), 2)
    score = with_halo(score_ref[...], 3)
    gain = jnp.exp2(label)
    disc = 1.0 / jnp.log2(1.0 + jnp.maximum(rank, 1.0))
    expo = jnp.exp(score)
    for slot, value in enumerate((query, gain, disc, expo)):
        rows[slot, 0 : blocks + 2, :] = value
        turned = value.T
        for b in range(blocks + 2):
            cols[slot, b * LANE : (b + 1) * LANE, :] = jnp.broadcast_to(
                turned[:, b : b + 1], (LANE, LANE)
            )
    grade = label.T
    turned = (
        jnp.where(grade >= 1.0, 1, 0)
        + jnp.where(grade >= 2.0, 1 << 8, 0)
        + jnp.where(grade >= 3.0, 1 << 16, 0)
        + jnp.where(grade >= 4.0, 1 << 24, 0)
    )
    for b in range(blocks + 2):
        packed_cols[b * LANE : (b + 1) * LANE, :] = jnp.broadcast_to(
            turned[:, b : b + 1], (LANE, LANE)
        )

    positions = iota((LANE, LANE), 0).astype(F32) + 1.0
    position_disc = 1.0 / jnp.log2(1.0 + positions)

    def one_block(b, carry):
        own_q = rows[0, pl.ds(b + 1, 1), :]
        own_g = rows[1, pl.ds(b + 1, 1), :]
        own_d = rows[2, pl.ds(b + 1, 1), :]
        own_e = rows[3, pl.ds(b + 1, 1), :]
        grad_sum = jnp.zeros((8, LANE), F32)
        hess_sum = jnp.zeros((8, LANE), F32)
        counts = jnp.zeros((8, LANE), jnp.int32)
        for chunk in range(3 * LANE // 8):
            at = pl.ds(pl.multiple_of(b * LANE + chunk * 8, 8), 8)
            far_e = cols[3, at, :]
            same = cols[0, at, :] == own_q
            gap = own_g - cols[1, at, :]
            signed = jnp.where(same, gap * jnp.abs(own_d - cols[2, at, :]), 0.0)
            inv = 1.0 / (own_e + far_e)
            scaled = signed * inv
            grad_sum = grad_sum + scaled * jnp.where(gap > 0.0, far_e, own_e)
            hess_sum = hess_sum + jnp.abs(scaled) * (far_e * inv)
            counts = counts + jnp.where(same, packed_cols[at, :], 0)
        count = jnp.sum(counts, axis=0, keepdims=True)
        grad = jnp.sum(grad_sum, axis=0, keepdims=True)
        hess = jnp.sum(hess_sum, axis=0, keepdims=True) * own_e
        ideal = jnp.zeros((LANE, LANE), F32)
        for k in range(4):
            count_k = (lax.shift_right_logical(count, 8 * k) & 255).astype(F32)
            ideal = ideal + jnp.where(positions <= count_k, float(1 << k), 0.0)
        ideal = jnp.sum(ideal * position_disc, axis=0, keepdims=True)
        norm = 1.0 / jnp.maximum(ideal, 1.0)
        grad_ref[pl.ds(b, 1), :] = -norm * grad
        hess_rows[pl.ds(b, 1), :] = norm * hess
        return carry

    lax.fori_loop(0, blocks, one_block, 0)

    hess_all = lanes_of(hess_rows[...])
    grad_all = lanes_of(grad_ref[...])
    leaf_all = lanes_of(leaf_ref[...])
    weighted[...] = (x_ref[...].astype(F32).T * hess_all).astype(BF16)
    member = leaf_all == iota((LEAVES, n_rows), 0)
    member_low = jnp.where(member, 1.0, 0.0).astype(BF16)
    grad_low = jnp.where(member, grad_all, 0.0).astype(BF16)
    moment_s[...] = jnp.dot(grad_low, x_ref[...], preferred_element_type=F32)
    hsum_s[...] = lax.dot_general(
        member_low, weighted[...], (((1,), (1,)), ((), ())), preferred_element_type=F32
    )
    htot = jnp.sum(jnp.where(member, hess_all, 0.0), axis=1, keepdims=True)
    gtot = jnp.sum(jnp.where(member, grad_all, 0.0), axis=1, keepdims=True)
    lane_at = iota((LEAVES, LANE), 1)
    total_s[...] = jnp.where(lane_at == 0, htot, jnp.where(lane_at == 1, gtot, 0.0))

    down = iota((half, half), 0)
    across = iota((half, half), 1)

    def one_leaf(leaf, carry):
        mask = jnp.where(leaf_all == leaf, 1.0, 0.0).astype(BF16)
        gram = jnp.dot(weighted[...] * mask, x_ref[...], preferred_element_type=F32)
        corner = gram[half:, :half]
        mixed = jnp.where(down >= across, gram[:half, :half], gram[half:, half:])
        diagonal = jnp.sum(
            jnp.where(down == across, gram[half:, half:], 0.0), axis=0, keepdims=True
        )
        hs = hsum_s[pl.ds(leaf, 1), :]
        mo = moment_s[pl.ds(leaf, 1), :]
        to = total_s[pl.ds(leaf, 1), :]
        rest = jnp.zeros((EXTRA - 4, LANE), F32)
        extra0 = jnp.concatenate([diagonal, hs[:, :half], hs[:, half:], to, rest], axis=0)
        rest = jnp.zeros((EXTRA - 2, LANE), F32)
        extra1 = jnp.concatenate([mo[:, :half], mo[:, half:], rest], axis=0)
        keep_ref[leaf, :half, :] = jnp.where(core == 0, corner, mixed)
        send_ref[leaf, :half, :] = jnp.where(core == 0, mixed, corner)
        keep_ref[leaf, half:, :] = jnp.where(core == 0, extra0, extra1)
        send_ref[leaf, half:, :] = jnp.where(core == 0, extra1, extra0)
        return carry

    lax.fori_loop(0, LEAVES, one_leaf, 0)


def pair_gram(where, x, score, label, query, rank, leaf, before, after):
    blocks = score.shape[0]
    n_rows, feats = x.shape
    vmem = pl.BlockSpec(memory_space=pltpu.VMEM)
    high = feats // 2 + EXTRA
    part = jax.ShapeDtypeStruct((LEAVES, high, LANE), F32)
    return pl.pallas_call(
        pair_gram_kernel,
        out_shape=(jax.ShapeDtypeStruct((blocks, LANE), F32), part, part),
        in_specs=[pl.BlockSpec(memory_space=pltpu.SMEM)] + [vmem] * 8,
        out_specs=(vmem, vmem, vmem),
        scratch_shapes=[
            pltpu.VMEM((4, blocks + 8, LANE), F32),
            pltpu.VMEM((4, (blocks + 2) * LANE, LANE), F32),
            pltpu.VMEM(((blocks + 2) * LANE, LANE), jnp.int32),
            pltpu.VMEM((blocks, LANE), F32),
            pltpu.VMEM((feats, n_rows), BF16),
            pltpu.VMEM((LEAVES, feats), F32),
            pltpu.VMEM((LEAVES, feats), F32),
            pltpu.VMEM((LEAVES, LANE), F32),
        ],
        compiler_params=pltpu.CompilerParams(vmem_limit_bytes=VMEM_LIMIT),
    )(where, x, score, label, query, rank, leaf, before, after)


def eliminate(tiles, at, offset):
    size = tiles[at].shape[0]
    down = iota((size, LANE), 0)
    scale = jnp.ones((size, LANE), F32)
    for base in range(0, size, GROUP):
        first = offset + base
        columns = [
            jnp.broadcast_to(tiles[at][:, first + j : first + j + 1], (size, LANE))
            for j in range(GROUP)
        ]
        for j in range(GROUP):
            p = base + j
            inverse = 1.0 / columns[j][p : p + 1, :]
            scale = jnp.where(down == p, inverse, scale)
            factor = jnp.where(down == p, 0.0, columns[j]) * inverse
            for k in range(j + 1, GROUP):
                columns[k] = columns[k] - factor * columns[k][p : p + 1, :]
            tiles = [t if t is None else t - factor * t[p : p + 1, :] for t in tiles]
    return [t if t is None else t * scale for t in tiles]


def exact_dot(a, b):
    return jnp.dot(a, b, precision=lax.Precision.HIGHEST, preferred_element_type=F32)


def solve_kernel(where_ref, own_ref, other_ref, out_ref):
    core = where_ref[0]
    high = own_ref.shape[0]
    half = high - EXTRA
    feats = 2 * half
    copies = out_ref.shape[0]
    own = own_ref[...]
    other = other_ref[...]
    part0 = jnp.where(core == 0, own, other)
    part1 = jnp.where(core == 0, other, own)
    corner = part0[:half]
    mixed = part1[:half]
    turned = mixed.T
    down = iota((half, half), 0)
    across = iota((half, half), 1)
    diag_row = part0[half : half + 1]
    upper_left = jnp.where(down >= across, mixed, turned)
    lower_right = jnp.where(down < across, mixed, jnp.where(down > across, turned, diag_row))
    hs0 = part0[half + 1 : half + 2]
    hs1 = part0[half + 2 : half + 3]
    htot = part0[half + 3 : half + 4, 0:1]
    gtot = part0[half + 3 : half + 4, 1:2]
    inv_den = 1.0 / (htot + LAMBDA)
    rhs0 = hs0 * (gtot * inv_den) - part1[half : half + 1]
    rhs1 = hs1 * (gtot * inv_den) - part1[half + 1 : half + 2]
    columns = jnp.concatenate(
        [hs0, hs1, rhs0, rhs1, jnp.zeros((4, LANE), F32)], axis=0
    ).T
    hc0 = columns[:, 0:1] * inv_den
    hc1 = columns[:, 1:2] * inv_den
    eye = jnp.where(down == across, LAMBDA, 0.0)
    top = [
        upper_left + eye - hc0 * hs0,
        corner.T - hc0 * hs1,
        jnp.where(across == 0, columns[:, 2:3], 0.0),
    ]
    low = [
        corner - hc1 * hs0,
        lower_right + eye - hc1 * hs1,
        jnp.where(across == 0, columns[:, 3:4], 0.0),
    ]
    per_tile = LANE // STRIP
    count = feats // STRIP
    strips = []
    for s in range(count):
        source = top if s < per_tile else low
        start = (s % per_tile) * STRIP
        strips.append([t[start : start + STRIP] for t in source])
    for s in range(count):
        tile, offset = s // per_tile, (s % per_tile) * STRIP
        done = eliminate([None] * tile + strips[s][tile:], tile, offset)
        strips[s] = done
        solved = jnp.concatenate(done[tile:], axis=1)
        later = [s + 1] if s + 1 < count else []
        others = [i for i in range(count) if i not in (s, s + 1)]
        for group in (later, others):
            if not group:
                continue
            left = jnp.concatenate(
                [strips[i][tile][:, offset : offset + STRIP] for i in group], axis=0
            )
            change = exact_dot(left, solved)
            for q, i in enumerate(group):
                part = change[q * STRIP : (q + 1) * STRIP]
                strips[i] = [
                    t if n < tile else t - part[:, (n - tile) * LANE : (n - tile + 1) * LANE]
                    for n, t in enumerate(strips[i])
                ]
    right = [strips[s][2] for s in range(count)]
    w0 = jnp.concatenate(right[:per_tile], axis=0).T[0:1, :]
    w1 = jnp.concatenate(right[per_tile:], axis=0).T[0:1, :]
    dotted = jnp.sum(hs0 * w0 + hs1 * w1, axis=1, keepdims=True)
    intercept = -(gtot + dotted) * inv_den
    result = jnp.concatenate(
        [w0, w1, jnp.broadcast_to(intercept, (1, LANE)), jnp.zeros((1, LANE), F32)], axis=0
    )
    out_ref[...] = jnp.broadcast_to(result[None], (copies, 4, LANE))


def solve_leaf(where, own, other, copies):
    high = own.shape[0]
    vmem = pl.BlockSpec(memory_space=pltpu.VMEM)
    return pl.pallas_call(
        solve_kernel,
        out_shape=jax.ShapeDtypeStruct((copies, 4, LANE), F32),
        in_specs=[pl.BlockSpec(memory_space=pltpu.SMEM), vmem, vmem],
        out_specs=vmem,
        compiler_params=pltpu.CompilerParams(vmem_limit_bytes=VMEM_LIMIT),
    )(where, own, other)


def output_kernel(owners, x_ref, coef_ref, score_ref, leaf_ref, tree_ref, new_ref):
    low = jnp.concatenate([coef_ref[d, 0:1, :] for d in owners], axis=0)
    high = jnp.concatenate([coef_ref[d, 1:2, :] for d in owners], axis=0)
    shift = jnp.concatenate([coef_ref[d, 2:3, :] for d in owners], axis=0)[:, 0:1]
    coefs = jnp.concatenate([low, high], axis=1)
    top = coefs.astype(BF16)
    left = coefs - top.astype(F32)
    middle = left.astype(BF16)
    bottom = (left - middle.astype(F32)).astype(BF16)
    stacked = jnp.concatenate([top, middle, bottom], axis=0)
    parts = lax.dot_general(
        stacked, x_ref[...], (((1,), (1,)), ((), ())), preferred_element_type=F32
    )
    per_leaf = (
        parts[:LEAVES] + (parts[LEAVES : 2 * LEAVES] + parts[2 * LEAVES :])
    ) + shift
    leaf_all = lanes_of(leaf_ref[...])
    chosen = jnp.sum(
        jnp.where(leaf_all == iota(per_leaf.shape, 0), per_leaf, 0.0), axis=0, keepdims=True
    )
    for b in range(score_ref.shape[0]):
        piece = chosen[:, b * LANE : (b + 1) * LANE]
        tree_ref[b : b + 1, :] = piece
        new_ref[b : b + 1, :] = score_ref[b : b + 1, :] + SHRINKAGE * piece


def row_outputs(owners, x, coefs, score, leaf):
    vmem = pl.BlockSpec(memory_space=pltpu.VMEM)
    shape = jax.ShapeDtypeStruct(score.shape, F32)
    return pl.pallas_call(
        lambda *refs: output_kernel(owners, *refs),
        out_shape=(shape, shape),
        in_specs=[vmem] * 4,
        out_specs=(vmem, vmem),
        compiler_params=pltpu.CompilerParams(vmem_limit_bytes=VMEM_LIMIT),
    )(x, coefs, score, leaf)


def split_plan(docs, leaf_devices):
    cores = 2
    spread = leaf_devices // cores
    low_docs = 2 if docs % 2 == 0 else 1
    high_docs = docs // low_docs

    def device(high, low, across, core):
        return (high * low_docs + low) * leaf_devices + across * cores + core

    near = [
        [device(h, l, a, c) for l in range(low_docs) for a in range(spread)]
        for h in range(high_docs)
        for c in range(cores)
    ]
    far = [
        [device(h, l, a, c) for h in range(high_docs)]
        for l in range(low_docs)
        for a in range(spread)
        for c in range(cores)
    ]
    return near, far


def reduce_groups(parts, groups, leaf_of):
    size = len(groups[0])
    held = parts.shape[0]
    if held % size == 0:
        own = held // size
        arrived = lax.all_to_all(parts, AXES, 0, 0, axis_index_groups=groups, tiled=True)
        total = jnp.sum(arrived.reshape((size, own) + parts.shape[1:]), axis=0)
        for group in groups:
            for place, device in enumerate(group):
                leaf_of[device] = leaf_of[device][place * own : (place + 1) * own]
        return total
    return lax.psum(parts, AXES, axis_index_groups=groups)


def body(features, scores, labels, query_ids, ranks, leaf_ids):
    docs = lax.axis_size("doc")
    leaf_devices = lax.axis_size("leaf")
    devices = docs * leaf_devices
    n_rows = features.shape[0]
    me = lax.axis_index(AXES)
    where = jnp.stack(
        [me % 2, (me == 0).astype(jnp.int32), (me == devices - 1).astype(jnp.int32)]
    ).astype(jnp.int32)
    blocked = [
        v.reshape(n_rows // LANE, LANE) for v in (scores, labels, query_ids, ranks, leaf_ids)
    ]
    score, label, query, rank, leaf = blocked

    def edge(block):
        return jnp.stack(
            [
                query[block].astype(F32),
                label[block].astype(F32),
                rank[block].astype(F32),
                score[block],
            ]
        )

    ahead = [(i, i + 1) for i in range(devices - 1)]
    behind = [(i + 1, i) for i in range(devices - 1)]
    before = lax.ppermute(edge(n_rows // LANE - 1), AXES, ahead)
    after = lax.ppermute(edge(0), AXES, behind)

    grad, keep, send = pair_gram(
        where, features, score, label, query, rank, leaf, before, after
    )
    swap = [(i, i ^ 1) for i in range(devices)]
    mine = keep + lax.ppermute(send, AXES, swap)

    near, far = split_plan(docs, leaf_devices)
    leaf_of = [list(range(LEAVES)) for _ in range(devices)]
    mine = reduce_groups(mine, near, leaf_of)
    mine = reduce_groups(mine, far, leaf_of)
    mine = mine[0]
    other = lax.ppermute(mine, AXES, swap)
    coefs = solve_leaf(where, mine, other, devices)
    coefs = lax.all_to_all(coefs, AXES, 0, 0, tiled=True)
    owners = [leaf_of.index([l]) for l in range(LEAVES)]
    tree, fresh = row_outputs(owners, features, coefs, score, leaf)
    return grad.reshape(-1), tree.reshape(-1), fresh.reshape(-1)


def solution(mesh):
    rows = P(AXES)
    return jax.shard_map(
        body,
        mesh=mesh,
        in_specs=(P(AXES, None), rows, rows, rows, rows, rows),
        out_specs=(rows, rows, rows),
        check_vma=False,
    )
```

```python
import jax
import jax.numpy as jnp
import numpy as np
from jax import lax
from jax.experimental import pallas as pl
from jax.experimental.pallas import tpu as pltpu
from jax.sharding import PartitionSpec as P

LEAVES = 16
MAXQ = 128
LAMBDA = 1.0
SHRINKAGE = 0.1
AXES = ("doc", "leaf")
LANE = 128
EXTRA = 8
STRIP = 32
GROUP = 16
NEAR = tuple(range(0, 16, 2))
GATHER = ((0, 2, 1, 3), (0, 4, 8, 12))
UNROLL = 2
VMEM_LIMIT = 48 * 1024 * 1024
F32 = jnp.float32
BF16 = jnp.bfloat16


def iota(shape, dim):
    return lax.broadcasted_iota(jnp.int32, shape, dim)


def lanes_of(block_rows):
    return jnp.concatenate(
        [block_rows[b : b + 1, :] for b in range(block_rows.shape[0])], axis=1
    )


def position():
    return lax.axis_index("doc") * lax.axis_size("leaf") + lax.axis_index("leaf")


def slot_mask(me):
    return (me & 1) * 8 + ((me >> 2) & 3) * 2 + ((me >> 1) & 1)


def fetch(sources, places, sems):
    copies = [
        pltpu.make_async_copy(src, dst, sems.at[n])
        for n, (src, dst) in enumerate(zip(sources, places))
    ]
    for copy in copies:
        copy.start()
    return copies


def edge_kernel(
    query_hbm, label_hbm, rank_hbm, score_hbm, leaf_hbm,
    inner_ref, outer_ref, table_ref, query, label, rank, score, leaf, sems,
):
    odd = (position() & 1) == 1
    copies = fetch(
        (query_hbm, label_hbm, rank_hbm, score_hbm, leaf_hbm),
        (query, label, rank, score, leaf),
        sems,
    )
    blocks = query.shape[0]
    for copy in copies:
        copy.wait()
    for n, ref in enumerate((query, label, rank, score, leaf)):
        value = ref[...].astype(F32)
        table_ref[n] = value
        if n < 4:
            first, last = value[0:1, :], value[blocks - 1 : blocks, :]
            inner_ref[n : n + 1, :] = jnp.where(odd, first, last)
            outer_ref[n : n + 1, :] = jnp.where(odd, last, first)


def edges(query, label, rank, score, leaf):
    blocks = score.shape[0]
    anywhere = pl.BlockSpec(memory_space=pltpu.HBM)
    vmem = pl.BlockSpec(memory_space=pltpu.VMEM)
    edge = jax.ShapeDtypeStruct((4, LANE), F32)
    whole = pltpu.VMEM((blocks, LANE), jnp.int32)
    return pl.pallas_call(
        edge_kernel,
        out_shape=(edge, edge, jax.ShapeDtypeStruct((5, blocks, LANE), F32)),
        in_specs=[anywhere] * 5,
        out_specs=(vmem,) * 3,
        scratch_shapes=[whole, whole, whole, pltpu.VMEM((blocks, LANE), F32), whole]
        + [pltpu.SemaphoreType.DMA((5,))],
    )(query, label, rank, score, leaf)


def pair_tables(query, label, rank, score, rows, cols, packed_cols):
    count = query.shape[0]
    gain = jnp.exp2(label)
    disc = 1.0 / jnp.log2(1.0 + jnp.maximum(rank, 1.0))
    expo = jnp.exp(score)
    for slot, value in enumerate((query, gain, disc, expo)):
        rows[slot, 0:count, :] = value
        turned = value.T
        for b in range(count):
            cols[slot, b * LANE : (b + 1) * LANE, :] = jnp.broadcast_to(
                turned[:, b : b + 1], (LANE, LANE)
            )
    grade = label.T
    turned = (
        jnp.where(grade >= 1.0, 1, 0)
        + jnp.where(grade >= 2.0, 1 << 8, 0)
        + jnp.where(grade >= 3.0, 1 << 16, 0)
        + jnp.where(grade >= 4.0, 1 << 24, 0)
    )
    for b in range(count):
        packed_cols[b * LANE : (b + 1) * LANE, :] = jnp.broadcast_to(
            turned[:, b : b + 1], (LANE, LANE)
        )


def pair_block(own, start, rows, cols, packed_cols):
    positions = iota((LANE, LANE), 0).astype(F32) + 1.0
    position_disc = 1.0 / jnp.log2(1.0 + positions)
    own_q = rows[0, pl.ds(own, 1), :]
    own_g = rows[1, pl.ds(own, 1), :]
    own_d = rows[2, pl.ds(own, 1), :]
    own_e = rows[3, pl.ds(own, 1), :]
    grad_sum = jnp.zeros((8, LANE), F32)
    hess_sum = jnp.zeros((8, LANE), F32)
    counts = jnp.zeros((8, LANE), jnp.int32)
    for chunk in range(3 * LANE // 8):
        at = pl.ds(pl.multiple_of(start * LANE + chunk * 8, 8), 8)
        far_e = cols[3, at, :]
        same = cols[0, at, :] == own_q
        gap = own_g - cols[1, at, :]
        signed = jnp.where(same, gap * jnp.abs(own_d - cols[2, at, :]), 0.0)
        inv = 1.0 / (own_e + far_e)
        scaled = signed * inv
        grad_sum = grad_sum + scaled * jnp.where(gap > 0.0, far_e, own_e)
        hess_sum = hess_sum + jnp.abs(scaled) * (far_e * inv)
        counts = counts + jnp.where(same, packed_cols[at, :], 0)
    count = jnp.sum(counts, axis=0, keepdims=True)
    grad = jnp.sum(grad_sum, axis=0, keepdims=True)
    hess = jnp.sum(hess_sum, axis=0, keepdims=True) * own_e
    ideal = jnp.zeros((LANE, LANE), F32)
    for k in range(4):
        count_k = (lax.shift_right_logical(count, 8 * k) & 255).astype(F32)
        ideal = ideal + jnp.where(positions <= count_k, float(1 << k), 0.0)
    ideal = jnp.sum(ideal * position_disc, axis=0, keepdims=True)
    norm = 1.0 / jnp.maximum(ideal, 1.0)
    return -norm * grad, norm * hess


def leaf_sums(x, turned, hess_all, grad_all, leaf_all, weighted, moment_s, hsum_s, total_s):
    n_rows = leaf_all.shape[1]
    weighted[...] = (turned * hess_all).astype(BF16)
    member = leaf_all == iota((LEAVES, n_rows), 0)
    member_low = jnp.where(member, 1.0, 0.0).astype(BF16)
    grad_low = jnp.where(member, grad_all, 0.0).astype(BF16)
    moment_s[...] = jnp.dot(grad_low, x, preferred_element_type=F32)
    hsum_s[...] = lax.dot_general(
        member_low, weighted[...], (((1,), (1,)), ((), ())), preferred_element_type=F32
    )
    htot = jnp.sum(jnp.where(member, hess_all, 0.0), axis=1, keepdims=True)
    gtot = jnp.sum(jnp.where(member, grad_all, 0.0), axis=1, keepdims=True)
    lane_at = iota((LEAVES, LANE), 1)
    total_s[...] = jnp.where(lane_at == 0, htot, jnp.where(lane_at == 1, gtot, 0.0))


def pack_grams(x_ref, leaf_all, weighted, moment_s, hsum_s, total_s, out_ref, base):
    half = x_ref.shape[1] // 2
    mask = slot_mask(position())
    down = iota((half, half), 0)
    across = iota((half, half), 1)

    def one_slot(slot, carry):
        leaf = (slot + base) ^ mask
        chosen = jnp.where(leaf_all == leaf.astype(F32), 1.0, 0.0).astype(BF16)
        gram = jnp.dot(weighted[...] * chosen, x_ref[...], preferred_element_type=F32)
        out_ref[slot, 0:half, :] = gram[half:, :half]
        out_ref[slot, half : 2 * half, :] = jnp.where(
            down >= across, gram[:half, :half], gram[half:, half:]
        )
        diagonal = jnp.sum(
            jnp.where(down == across, gram[half:, half:], 0.0), axis=0, keepdims=True
        )
        hs = hsum_s[pl.ds(leaf, 1), :]
        mo = moment_s[pl.ds(leaf, 1), :]
        to = total_s[pl.ds(leaf, 1), :]
        out_ref[slot, 2 * half :, :] = jnp.concatenate(
            [diagonal, hs[:, :half], hs[:, half:], mo[:, :half], mo[:, half:], to]
            + [jnp.zeros((EXTRA - 6, LANE), F32)],
            axis=0,
        )
        return carry

    lax.fori_loop(0, out_ref.shape[0], one_slot, 0, unroll=UNROLL)


def interior_kernel(table, grad_ref, hess_ref, rows, cols, packed_cols):
    blocks = grad_ref.shape[0]
    pair_tables(table[0], table[1], table[2], table[3], rows, cols, packed_cols)
    nothing = jnp.zeros((1, LANE), F32)
    for ref in (grad_ref, hess_ref):
        ref[0:1, :] = nothing
        ref[blocks - 1 : blocks, :] = nothing

    def one_block(b, carry):
        grad, hess = pair_block(b, b - 1, rows, cols, packed_cols)
        grad_ref[pl.ds(b, 1), :] = grad
        hess_ref[pl.ds(b, 1), :] = hess
        return carry

    lax.fori_loop(1, blocks - 1, one_block, 0)


def boundary_kernel(
    table, x_ref, inner, outer, grad_part, hess_part,
    grad_ref, send_ref, weighted, moment_s, hsum_s, total_s, x_out,
    rows, cols, packed_cols,
):
    blocks = grad_ref.shape[0]
    final = blocks - 1
    me = position()
    devices = lax.axis_size("doc") * lax.axis_size("leaf")

    odd = (me & 1) == 1

    def window(slot):
        near = inner[slot : slot + 1, :]
        far = outer[slot : slot + 1, :]
        return jnp.concatenate(
            [
                jnp.where(odd, near, far),
                table[slot, 0:2, :],
                table[slot, final - 1 :, :],
                jnp.where(odd, far, near),
            ],
            axis=0,
        )

    ids = window(0)
    at = iota(ids.shape, 0)
    outside = ((at == 0) & (me == 0)) | ((at == 5) & (me == devices - 1))
    pair_tables(
        jnp.where(outside, -1.0, ids), window(1), window(2), window(3), rows, cols, packed_cols
    )
    head_grad, head_hess = pair_block(1, 0, rows, cols, packed_cols)
    tail_grad, tail_hess = pair_block(4, 3, rows, cols, packed_cols)
    grads = jnp.concatenate([head_grad, grad_part[1:final, :], tail_grad], axis=0)
    hesses = jnp.concatenate([head_hess, hess_part[1:final, :], tail_hess], axis=0)
    grad_ref[...] = grads
    x_out[...] = x_ref[...]
    leaf_all = lanes_of(table[4])
    leaf_sums(
        x_ref[...], x_ref[...].astype(F32).T, lanes_of(hesses), lanes_of(grads), leaf_all,
        weighted, moment_s, hsum_s, total_s,
    )
    pack_grams(x_ref, leaf_all, weighted, moment_s, hsum_s, total_s, send_ref, LEAVES // 2)


def keep_kernel(table, x_ref, weighted, moment_s, hsum_s, total_s, keep_ref):
    pack_grams(
        x_ref, lanes_of(table[4]), weighted, moment_s, hsum_s, total_s, keep_ref, 0
    )


def table_scratch(count):
    return [
        pltpu.VMEM((4, 8 * pl.cdiv(count, 8), LANE), F32),
        pltpu.VMEM((4, count * LANE, LANE), F32),
        pltpu.VMEM((count * LANE, LANE), jnp.int32),
    ]


def on_chip(kernel, outs, scratch, args, cost=None):
    vmem = pl.BlockSpec(memory_space=pltpu.VMEM)
    return pl.pallas_call(
        kernel,
        out_shape=tuple(jax.ShapeDtypeStruct(shape, kind) for shape, kind in outs),
        in_specs=[vmem] * len(args),
        out_specs=(vmem,) * len(outs),
        scratch_shapes=scratch,
        compiler_params=pltpu.CompilerParams(vmem_limit_bytes=VMEM_LIMIT),
        cost_estimate=cost,
    )(*args)


def interior(table):
    _, blocks, _ = table.shape
    cost = pl.CostEstimate(
        flops=20000 * blocks * LANE * LANE, bytes_accessed=blocks * LANE * LANE, transcendentals=0
    )
    row = ((blocks, LANE), F32)
    return on_chip(interior_kernel, (row, row), table_scratch(blocks), (table,), cost)


def boundary(table, x, inner, outer, grad, hess):
    n_rows, feats = x.shape
    outs = (
        (grad.shape, F32),
        ((LEAVES // 2, feats + EXTRA, LANE), F32),
        ((feats, n_rows), BF16),
        ((LEAVES, feats), F32),
        ((LEAVES, feats), F32),
        ((LEAVES, LANE), F32),
        (x.shape, x.dtype),
    )
    return on_chip(
        boundary_kernel, outs, table_scratch(6), (table, x, inner, outer, grad, hess)
    )


def keep_part(table, x, weighted, moment, hsum, totals):
    n_rows, feats = x.shape
    cost = pl.CostEstimate(
        flops=LEAVES * n_rows * feats * feats, bytes_accessed=4 * n_rows * feats, transcendentals=0
    )
    outs = (((LEAVES // 2, feats + EXTRA, LANE), F32),)
    return on_chip(keep_kernel, outs, [], (table, x, weighted, moment, hsum, totals), cost)[0]


def fold_kernel(keep_ref, other_ref, *outs):
    for n, out in enumerate(outs):
        out[...] = keep_ref[n] + other_ref[n]


def fold(keep, other):
    return on_chip(fold_kernel, ((keep.shape[1:], F32),) * keep.shape[0], [], (keep, other))


def tree_sum(values):
    while len(values) > 1:
        values = [a + b for a, b in zip(values[::2], values[1::2])]
    return values[0]


def total_kernel(*refs):
    refs[-1][...] = tree_sum([ref[...] for ref in refs[:-1]])


def total(parts):
    return on_chip(total_kernel, ((parts[0].shape, F32),), [], parts)[0]


def eliminate(tiles, at, offset):
    size = tiles[at].shape[0]
    down = iota((size, LANE), 0)
    scale = jnp.ones((size, LANE), F32)
    for base in range(0, size, GROUP):
        first = offset + base
        columns = [
            jnp.broadcast_to(tiles[at][:, first + j : first + j + 1], (size, LANE))
            for j in range(GROUP)
        ]
        for j in range(GROUP):
            p = base + j
            inverse = 1.0 / columns[j][p : p + 1, :]
            scale = jnp.where(down == p, inverse, scale)
            factor = jnp.where(down == p, 0.0, columns[j]) * inverse
            for k in range(j + 1, GROUP):
                columns[k] = columns[k] - factor * columns[k][p : p + 1, :]
            tiles = [t if t is None else t - factor * t[p : p + 1, :] for t in tiles]
    return [t if t is None else t * scale for t in tiles]


def exact_dot(a, b):
    return jnp.dot(a, b, precision=lax.Precision.HIGHEST, preferred_element_type=F32)


def solve_kernel(*refs):
    ins, out_ref = refs[:-1], refs[-1]
    summed = tree_sum([ref[...] for ref in ins])
    feats = summed.shape[0] - EXTRA
    half = feats // 2
    corner = summed[:half]
    mixed = summed[half:feats]
    extra = [summed[feats + n : feats + n + 1] for n in range(6)]
    turned = mixed.T
    down = iota((half, half), 0)
    across = iota((half, half), 1)
    diag_row, hs0, hs1, mo0, mo1, totals = extra
    upper_left = jnp.where(down >= across, mixed, turned)
    lower_right = jnp.where(down < across, mixed, jnp.where(down > across, turned, diag_row))
    htot = totals[:, 0:1]
    gtot = totals[:, 1:2]
    inv_den = 1.0 / (htot + LAMBDA)
    rhs0 = hs0 * (gtot * inv_den) - mo0
    rhs1 = hs1 * (gtot * inv_den) - mo1
    columns = jnp.concatenate(
        [hs0, hs1, rhs0, rhs1, jnp.zeros((4, LANE), F32)], axis=0
    ).T
    hc0 = columns[:, 0:1] * inv_den
    hc1 = columns[:, 1:2] * inv_den
    eye = jnp.where(down == across, LAMBDA, 0.0)
    top = [
        upper_left + eye - hc0 * hs0,
        corner.T - hc0 * hs1,
        jnp.where(across == 0, columns[:, 2:3], 0.0),
    ]
    low = [
        corner - hc1 * hs0,
        lower_right + eye - hc1 * hs1,
        jnp.where(across == 0, columns[:, 3:4], 0.0),
    ]
    per_tile = LANE // STRIP
    count = feats // STRIP
    strips = []
    for s in range(count):
        source = top if s < per_tile else low
        start = (s % per_tile) * STRIP
        strips.append([t[start : start + STRIP] for t in source])
    for s in range(count):
        tile, offset = s // per_tile, (s % per_tile) * STRIP
        done = eliminate([None] * tile + strips[s][tile:], tile, offset)
        strips[s] = done
        solved = jnp.concatenate(done[tile:], axis=1)
        later = [s + 1] if s + 1 < count else []
        others = [i for i in range(count) if i not in (s, s + 1)]
        for group in (later, others):
            if not group:
                continue
            left = jnp.concatenate(
                [strips[i][tile][:, offset : offset + STRIP] for i in group], axis=0
            )
            change = exact_dot(left, solved)
            for q, i in enumerate(group):
                part = change[q * STRIP : (q + 1) * STRIP]
                strips[i] = [
                    t if n < tile else t - part[:, (n - tile) * LANE : (n - tile + 1) * LANE]
                    for n, t in enumerate(strips[i])
                ]
    right = [strips[s][2] for s in range(count)]
    w0 = jnp.concatenate(right[:per_tile], axis=0).T[0:1, :]
    w1 = jnp.concatenate(right[per_tile:], axis=0).T[0:1, :]
    dotted = jnp.sum(hs0 * w0 + hs1 * w1, axis=1, keepdims=True)
    intercept = -(gtot + dotted) * inv_den
    out_ref[...] = jnp.concatenate(
        [w0, w1, jnp.broadcast_to(intercept, (1, LANE)), jnp.zeros((1, LANE), F32)], axis=0
    )


def solve_leaf(parts):
    return on_chip(solve_kernel, (((4, LANE), F32),), [], parts)[0]


def output_kernel(table, x_ref, c0, c1, c2, c3, tree_ref, new_ref):
    groups = (c0, c1, c2, c3)
    slots = [groups[n >> 1 & 3][(n >> 3) * 2 + (n & 1)] for n in range(LEAVES)]
    low = jnp.concatenate([c[0:1, :] for c in slots], axis=0)
    high = jnp.concatenate([c[1:2, :] for c in slots], axis=0)
    shift = jnp.concatenate([c[2:3, :] for c in slots], axis=0)[:, 0:1]
    coefs = jnp.concatenate([low, high], axis=1)
    top = coefs.astype(BF16)
    left = coefs - top.astype(F32)
    middle = left.astype(BF16)
    bottom = (left - middle.astype(F32)).astype(BF16)
    stacked = jnp.concatenate([top, middle, bottom], axis=0)
    parts = lax.dot_general(
        stacked, x_ref[...], (((1,), (1,)), ((), ())), preferred_element_type=F32
    )
    per_leaf = (
        parts[:LEAVES] + (parts[LEAVES : 2 * LEAVES] + parts[2 * LEAVES :])
    ) + shift
    leaf_all = lanes_of(table[4])
    leaf_at = (iota(per_leaf.shape, 0) ^ slot_mask(position())).astype(F32)
    chosen = jnp.sum(jnp.where(leaf_all == leaf_at, per_leaf, 0.0), axis=0, keepdims=True)
    for b in range(tree_ref.shape[0]):
        piece = chosen[:, b * LANE : (b + 1) * LANE]
        tree_ref[b : b + 1, :] = piece
        new_ref[b : b + 1, :] = table[3, b : b + 1, :] + SHRINKAGE * piece


def row_outputs(table, x, coefs):
    row = (table.shape[1:], F32)
    return on_chip(output_kernel, (row, row), [], (table, x, *coefs))


def body(features, scores, labels, query_ids, ranks, leaf_ids):
    devices = lax.axis_size("doc") * lax.axis_size("leaf")
    n_rows = features.shape[0]
    score, label, query, rank, leaf = [
        v.reshape(n_rows // LANE, LANE) for v in (scores, labels, query_ids, ranks, leaf_ids)
    ]

    def swapped(value, flip):
        return lax.ppermute(value, AXES, [(i, i ^ flip) for i in range(devices)])

    x = features
    inner, outer, table = edges(query, label, rank, score, leaf)
    inner = swapped(inner, 1)
    outer = lax.ppermute(
        outer, AXES, [p for i in range(1, devices - 1, 2) for p in ((i, i + 1), (i + 1, i))]
    )
    grad, hess = interior(table)
    grad, send, *sums, held = boundary(table, x, inner, outer, grad, hess)
    other = swapped(send, 1)
    chunks = fold(keep_part(table, held, *sums), other)
    mine = total([swapped(c, flip) if flip else c for c, flip in zip(chunks, NEAR)])
    parts = [mine, swapped(mine, 16)]
    bit = 32
    while bit < devices:
        mine = parts[0] + parts[1]
        parts = [mine, swapped(mine, bit)]
        bit *= 2
    coefs = solve_leaf(parts)
    group = jnp.stack([swapped(coefs, flip) if flip else coefs for flip in GATHER[0]])
    coefs = [swapped(group, flip) if flip else group for flip in GATHER[1]]
    tree, fresh = row_outputs(table, x, coefs)
    return grad.reshape(-1), tree.reshape(-1), fresh.reshape(-1)


def solution(mesh):
    rows = P(AXES)
    return jax.shard_map(
        body,
        mesh=mesh,
        in_specs=(P(AXES, None), rows, rows, rows, rows, rows),
        out_specs=(rows, rows, rows),
        check_vma=False,
    )
```

```python
import functools

import jax
import jax.numpy as jnp
import numpy as np
from jax import lax
from jax.experimental import pallas as pl
from jax.experimental.pallas import tpu as pltpu
from jax.sharding import PartitionSpec as P

LEAVES = 16
MAXQ = 128
LAMBDA = 1.0
SHRINKAGE = 0.1
AXES = ("doc", "leaf")
LANE = 128
EXTRA = 8
STRIP = 32
GROUP = 16
NEAR = ((0, 4, 2, 1), (7, 6, 5, 3))
GATHER = ((0, 2, 1, 3), (0, 4, 8, 12))
PART = 4
VMEM_LIMIT = 48 * 1024 * 1024
F32 = jnp.float32
BF16 = jnp.bfloat16


def iota(shape, dim):
    return lax.broadcasted_iota(jnp.int32, shape, dim)


def lanes_of(block_rows):
    return jnp.concatenate(
        [block_rows[b : b + 1, :] for b in range(block_rows.shape[0])], axis=1
    )


def position():
    return lax.axis_index("doc") * lax.axis_size("leaf") + lax.axis_index("leaf")


def slot_mask(me):
    return (me & 1) * 8 + ((me >> 2) & 3) * 2 + ((me >> 1) & 1)


def other_core(codes):
    return tuple(code + LEAVES // 2 for code in codes)


def fetch(sources, places, sems):
    copies = [
        pltpu.make_async_copy(src, dst, sems.at[n])
        for n, (src, dst) in enumerate(zip(sources, places))
    ]
    for copy in copies:
        copy.start()
    return copies


def edge_kernel(
    query_hbm, label_hbm, rank_hbm, score_hbm, leaf_hbm,
    inner_ref, outer_ref, table_ref, query, label, rank, score, leaf, sems,
):
    odd = (position() & 1) == 1
    copies = fetch(
        (query_hbm, label_hbm, rank_hbm, score_hbm, leaf_hbm),
        (query, label, rank, score, leaf),
        sems,
    )
    blocks = query.shape[0]
    for copy in copies:
        copy.wait()
    for n, ref in enumerate((query, label, rank, score, leaf)):
        value = ref[...].astype(F32)
        table_ref[n] = value
        if n < 4:
            first, last = value[0:1, :], value[blocks - 1 : blocks, :]
            inner_ref[n : n + 1, :] = jnp.where(odd, first, last)
            outer_ref[n : n + 1, :] = jnp.where(odd, last, first)


def edges(query, label, rank, score, leaf):
    blocks = score.shape[0]
    anywhere = pl.BlockSpec(memory_space=pltpu.HBM)
    vmem = pl.BlockSpec(memory_space=pltpu.VMEM)
    edge = jax.ShapeDtypeStruct((4, LANE), F32)
    whole = pltpu.VMEM((blocks, LANE), jnp.int32)
    return pl.pallas_call(
        edge_kernel,
        out_shape=(edge, edge, jax.ShapeDtypeStruct((5, blocks, LANE), F32)),
        in_specs=[anywhere] * 5,
        out_specs=(vmem,) * 3,
        scratch_shapes=[whole, whole, whole, pltpu.VMEM((blocks, LANE), F32), whole]
        + [pltpu.SemaphoreType.DMA((5,))],
    )(query, label, rank, score, leaf)


def pair_tables(query, label, rank, score, rows, cols, packed_cols):
    count = query.shape[0]
    gain = jnp.exp2(label)
    disc = 1.0 / jnp.log2(1.0 + jnp.maximum(rank, 1.0))
    expo = jnp.exp(score)
    for slot, value in enumerate((query, gain, disc, expo)):
        rows[slot, 0:count, :] = value
        turned = value.T
        for b in range(count):
            cols[slot, b * LANE : (b + 1) * LANE, :] = jnp.broadcast_to(
                turned[:, b : b + 1], (LANE, LANE)
            )
    grade = label.T
    turned = (
        jnp.where(grade >= 1.0, 1, 0)
        + jnp.where(grade >= 2.0, 1 << 8, 0)
        + jnp.where(grade >= 3.0, 1 << 16, 0)
        + jnp.where(grade >= 4.0, 1 << 24, 0)
    )
    for b in range(count):
        packed_cols[b * LANE : (b + 1) * LANE, :] = jnp.broadcast_to(
            turned[:, b : b + 1], (LANE, LANE)
        )


def pair_block(own, start, rows, cols, packed_cols):
    positions = iota((LANE, LANE), 0).astype(F32) + 1.0
    position_disc = 1.0 / jnp.log2(1.0 + positions)
    own_q = rows[0, pl.ds(own, 1), :]
    own_g = rows[1, pl.ds(own, 1), :]
    own_d = rows[2, pl.ds(own, 1), :]
    own_e = rows[3, pl.ds(own, 1), :]
    grad_sum = jnp.zeros((8, LANE), F32)
    hess_sum = jnp.zeros((8, LANE), F32)
    counts = jnp.zeros((8, LANE), jnp.int32)
    for chunk in range(3 * LANE // 8):
        at = pl.ds(pl.multiple_of(start * LANE + chunk * 8, 8), 8)
        far_e = cols[3, at, :]
        same = cols[0, at, :] == own_q
        gap = own_g - cols[1, at, :]
        signed = jnp.where(same, gap * jnp.abs(own_d - cols[2, at, :]), 0.0)
        inv = 1.0 / (own_e + far_e)
        scaled = signed * inv
        grad_sum = grad_sum + scaled * jnp.where(gap > 0.0, far_e, own_e)
        hess_sum = hess_sum + jnp.abs(scaled) * (far_e * inv)
        counts = counts + jnp.where(same, packed_cols[at, :], 0)
    count = jnp.sum(counts, axis=0, keepdims=True)
    grad = jnp.sum(grad_sum, axis=0, keepdims=True)
    hess = jnp.sum(hess_sum, axis=0, keepdims=True) * own_e
    ideal = jnp.zeros((LANE, LANE), F32)
    for k in range(4):
        count_k = (lax.shift_right_logical(count, 8 * k) & 255).astype(F32)
        ideal = ideal + jnp.where(positions <= count_k, float(1 << k), 0.0)
    ideal = jnp.sum(ideal * position_disc, axis=0, keepdims=True)
    norm = 1.0 / jnp.maximum(ideal, 1.0)
    return -norm * grad, norm * hess


def leaf_sums(x, turned, hess_all, grad_all, leaf_all, weighted, moment_s, hsum_s, total_s):
    n_rows = leaf_all.shape[1]
    weighted[...] = (turned * hess_all).astype(BF16)
    member = leaf_all == iota((LEAVES, n_rows), 0)
    member_low = jnp.where(member, 1.0, 0.0).astype(BF16)
    grad_low = jnp.where(member, grad_all, 0.0).astype(BF16)
    moment_s[...] = jnp.dot(grad_low, x, preferred_element_type=F32)
    hsum_s[...] = lax.dot_general(
        member_low, weighted[...], (((1,), (1,)), ((), ())), preferred_element_type=F32
    )
    htot = jnp.sum(jnp.where(member, hess_all, 0.0), axis=1, keepdims=True)
    gtot = jnp.sum(jnp.where(member, grad_all, 0.0), axis=1, keepdims=True)
    lane_at = iota((LEAVES, LANE), 1)
    total_s[...] = jnp.where(lane_at == 0, htot, jnp.where(lane_at == 1, gtot, 0.0))


def pack_grams(x_ref, leaf_all, weighted, moment_s, hsum_s, total_s, out_ref, codes):
    half = x_ref.shape[1] // 2
    mask = slot_mask(position())
    down = iota((half, half), 0)
    across = iota((half, half), 1)

    for slot, code in enumerate(codes):
        leaf = mask ^ code
        chosen = jnp.where(leaf_all == leaf.astype(F32), 1.0, 0.0).astype(BF16)
        gram = jnp.dot(weighted[...] * chosen, x_ref[...], preferred_element_type=F32)
        out_ref[slot, 0:half, :] = gram[half:, :half]
        out_ref[slot, half : 2 * half, :] = jnp.where(
            down >= across, gram[:half, :half], gram[half:, half:]
        )
        diagonal = jnp.sum(
            jnp.where(down == across, gram[half:, half:], 0.0), axis=0, keepdims=True
        )
        hs = hsum_s[pl.ds(leaf, 1), :]
        mo = moment_s[pl.ds(leaf, 1), :]
        to = total_s[pl.ds(leaf, 1), :]
        out_ref[slot, 2 * half :, :] = jnp.concatenate(
            [diagonal, hs[:, :half], hs[:, half:], mo[:, :half], mo[:, half:], to]
            + [jnp.zeros((EXTRA - 6, LANE), F32)],
            axis=0,
        )


def interior_kernel(table, grad_ref, hess_ref, rows, cols, packed_cols):
    blocks = grad_ref.shape[0]
    pair_tables(table[0], table[1], table[2], table[3], rows, cols, packed_cols)
    nothing = jnp.zeros((1, LANE), F32)
    for ref in (grad_ref, hess_ref):
        ref[0:1, :] = nothing
        ref[blocks - 1 : blocks, :] = nothing

    def one_block(b, carry):
        grad, hess = pair_block(b, b - 1, rows, cols, packed_cols)
        grad_ref[pl.ds(b, 1), :] = grad
        hess_ref[pl.ds(b, 1), :] = hess
        return carry

    lax.fori_loop(1, blocks - 1, one_block, 0)


def boundary_kernel(
    table, x_ref, inner, outer, grad_part, hess_part,
    grad_ref, send_ref, weighted, moment_s, hsum_s, total_s, x_out,
    rows, cols, packed_cols,
):
    blocks = grad_ref.shape[0]
    final = blocks - 1
    me = position()
    devices = lax.axis_size("doc") * lax.axis_size("leaf")

    odd = (me & 1) == 1

    def window(slot):
        near = inner[slot : slot + 1, :]
        far = outer[slot : slot + 1, :]
        return jnp.concatenate(
            [
                jnp.where(odd, near, far),
                table[slot, 0:2, :],
                table[slot, final - 1 :, :],
                jnp.where(odd, far, near),
            ],
            axis=0,
        )

    ids = window(0)
    at = iota(ids.shape, 0)
    outside = ((at == 0) & (me == 0)) | ((at == 5) & (me == devices - 1))
    pair_tables(
        jnp.where(outside, -1.0, ids), window(1), window(2), window(3), rows, cols, packed_cols
    )
    head_grad, head_hess = pair_block(1, 0, rows, cols, packed_cols)
    tail_grad, tail_hess = pair_block(4, 3, rows, cols, packed_cols)
    grads = jnp.concatenate([head_grad, grad_part[1:final, :], tail_grad], axis=0)
    hesses = jnp.concatenate([head_hess, hess_part[1:final, :], tail_hess], axis=0)
    grad_ref[...] = grads
    x_out[...] = x_ref[...]
    leaf_all = lanes_of(table[4])
    leaf_sums(
        x_ref[...], x_ref[...].astype(F32).T, lanes_of(hesses), lanes_of(grads), leaf_all,
        weighted, moment_s, hsum_s, total_s,
    )
    pack_grams(x_ref, leaf_all, weighted, moment_s, hsum_s, total_s, send_ref, other_core(NEAR[0]))


def gram_kernel(codes, table, x_ref, weighted, moment_s, hsum_s, total_s, out_ref):
    pack_grams(
        x_ref, lanes_of(table[4]), weighted, moment_s, hsum_s, total_s, out_ref, codes
    )


def table_scratch(count):
    return [
        pltpu.VMEM((4, 8 * pl.cdiv(count, 8), LANE), F32),
        pltpu.VMEM((4, count * LANE, LANE), F32),
        pltpu.VMEM((count * LANE, LANE), jnp.int32),
    ]


def on_chip(kernel, outs, scratch, args, cost=None):
    vmem = pl.BlockSpec(memory_space=pltpu.VMEM)
    return pl.pallas_call(
        kernel,
        out_shape=tuple(jax.ShapeDtypeStruct(shape, kind) for shape, kind in outs),
        in_specs=[vmem] * len(args),
        out_specs=(vmem,) * len(outs),
        scratch_shapes=scratch,
        compiler_params=pltpu.CompilerParams(vmem_limit_bytes=VMEM_LIMIT),
        cost_estimate=cost,
    )(*args)


def interior(table):
    _, blocks, _ = table.shape
    cost = pl.CostEstimate(
        flops=20000 * blocks * LANE * LANE, bytes_accessed=blocks * LANE * LANE, transcendentals=0
    )
    row = ((blocks, LANE), F32)
    return on_chip(interior_kernel, (row, row), table_scratch(blocks), (table,), cost)


def boundary(table, x, inner, outer, grad, hess):
    n_rows, feats = x.shape
    outs = (
        (grad.shape, F32),
        ((PART, feats + EXTRA, LANE), F32),
        ((feats, n_rows), BF16),
        ((LEAVES, feats), F32),
        ((LEAVES, feats), F32),
        ((LEAVES, LANE), F32),
        (x.shape, x.dtype),
    )
    return on_chip(
        boundary_kernel, outs, table_scratch(6), (table, x, inner, outer, grad, hess)
    )


def gram_part(codes, table, x, weighted, moment, hsum, totals):
    n_rows, feats = x.shape
    cost = pl.CostEstimate(
        flops=8 * PART * n_rows * feats * feats, bytes_accessed=n_rows * feats, transcendentals=0
    )
    outs = (((PART, feats + EXTRA, LANE), F32),)
    kernel = functools.partial(gram_kernel, codes)
    return on_chip(kernel, outs, [], (table, x, weighted, moment, hsum, totals), cost)[0]


def fold_kernel(keep_ref, other_ref, *outs):
    for n, out in enumerate(outs):
        out[...] = keep_ref[n] + other_ref[n]


def fold(keep, other):
    return on_chip(fold_kernel, ((keep.shape[1:], F32),) * keep.shape[0], [], (keep, other))


def tree_sum(values):
    while len(values) > 1:
        values = [a + b for a, b in zip(values[::2], values[1::2])]
    return values[0]


def total_kernel(*refs):
    refs[-1][...] = tree_sum([ref[...] for ref in refs[:-1]])


def total(parts):
    return on_chip(total_kernel, ((parts[0].shape, F32),), [], parts)[0]


def eliminate(tiles, at, offset):
    size = tiles[at].shape[0]
    down = iota((size, LANE), 0)
    scale = jnp.ones((size, LANE), F32)
    for base in range(0, size, GROUP):
        first = offset + base
        columns = [
            jnp.broadcast_to(tiles[at][:, first + j : first + j + 1], (size, LANE))
            for j in range(GROUP)
        ]
        for j in range(GROUP):
            p = base + j
            inverse = 1.0 / columns[j][p : p + 1, :]
            scale = jnp.where(down == p, inverse, scale)
            factor = jnp.where(down == p, 0.0, columns[j]) * inverse
            for k in range(j + 1, GROUP):
                columns[k] = columns[k] - factor * columns[k][p : p + 1, :]
            tiles = [t if t is None else t - factor * t[p : p + 1, :] for t in tiles]
    return [t if t is None else t * scale for t in tiles]


def three(value):
    top = value.astype(BF16)
    left = value - top.astype(F32)
    middle = left.astype(BF16)
    return top, middle, (left - middle.astype(F32)).astype(BF16)


def left_parts(value):
    top, middle, bottom = three(value)
    return jnp.concatenate([top, top, middle, top, middle, bottom], axis=1)


def right_parts(value):
    top, middle, bottom = three(value)
    return jnp.concatenate([top, middle, top, bottom, middle, top], axis=0)


def solve_kernel(*refs):
    ins, out_ref = refs[:-1], refs[-1]
    summed = tree_sum([ref[...] for ref in ins])
    feats = summed.shape[0] - EXTRA
    half = feats // 2
    corner = summed[:half]
    mixed = summed[half:feats]
    extra = [summed[feats + n : feats + n + 1] for n in range(6)]
    turned = mixed.T
    down = iota((half, half), 0)
    across = iota((half, half), 1)
    diag_row, hs0, hs1, mo0, mo1, totals = extra
    upper_left = jnp.where(down >= across, mixed, turned)
    lower_right = jnp.where(down < across, mixed, jnp.where(down > across, turned, diag_row))
    htot = totals[:, 0:1]
    gtot = totals[:, 1:2]
    inv_den = 1.0 / (htot + LAMBDA)
    rhs0 = hs0 * (gtot * inv_den) - mo0
    rhs1 = hs1 * (gtot * inv_den) - mo1
    columns = jnp.concatenate(
        [hs0, hs1, rhs0, rhs1, jnp.zeros((4, LANE), F32)], axis=0
    ).T
    hc0 = columns[:, 0:1] * inv_den
    hc1 = columns[:, 1:2] * inv_den
    eye = jnp.where(down == across, LAMBDA, 0.0)
    top = [
        upper_left + eye - hc0 * hs0,
        corner.T - hc0 * hs1,
        jnp.where(across == 0, columns[:, 2:3], 0.0),
    ]
    low = [
        corner - hc1 * hs0,
        lower_right + eye - hc1 * hs1,
        jnp.where(across == 0, columns[:, 3:4], 0.0),
    ]
    per_tile = LANE // STRIP
    count = feats // STRIP
    strips = []
    for s in range(count):
        source = top if s < per_tile else low
        start = (s % per_tile) * STRIP
        strips.append([t[start : start + STRIP] for t in source])
    for s in range(count):
        tile, offset = s // per_tile, (s % per_tile) * STRIP
        done = eliminate([None] * tile + strips[s][tile:], tile, offset)
        strips[s] = done
        solved = right_parts(jnp.concatenate(done[tile:], axis=1))
        later = [s + 1] if s + 1 < count else []
        others = [i for i in range(count) if i not in (s, s + 1)]
        for group in (later, others):
            if not group:
                continue
            left = jnp.concatenate(
                [strips[i][tile][:, offset : offset + STRIP] for i in group], axis=0
            )
            change = jnp.dot(left_parts(left), solved, preferred_element_type=F32)
            for q, i in enumerate(group):
                part = change[q * STRIP : (q + 1) * STRIP]
                strips[i] = [
                    t if n < tile else t - part[:, (n - tile) * LANE : (n - tile + 1) * LANE]
                    for n, t in enumerate(strips[i])
                ]
    right = [strips[s][2] for s in range(count)]
    w0 = jnp.concatenate(right[:per_tile], axis=0).T[0:1, :]
    w1 = jnp.concatenate(right[per_tile:], axis=0).T[0:1, :]
    dotted = jnp.sum(hs0 * w0 + hs1 * w1, axis=1, keepdims=True)
    intercept = -(gtot + dotted) * inv_den
    out_ref[...] = jnp.concatenate(
        [w0, w1, jnp.broadcast_to(intercept, (1, LANE)), jnp.zeros((1, LANE), F32)], axis=0
    )


def solve_leaf(parts):
    return on_chip(solve_kernel, (((4, LANE), F32),), [], parts)[0]


def output_kernel(table, x_ref, c0, c1, c2, c3, tree_ref, new_ref):
    groups = (c0, c1, c2, c3)
    slots = [groups[n >> 1 & 3][(n >> 3) * 2 + (n & 1)] for n in range(LEAVES)]
    low = jnp.concatenate([c[0:1, :] for c in slots], axis=0)
    high = jnp.concatenate([c[1:2, :] for c in slots], axis=0)
    shift = jnp.concatenate([c[2:3, :] for c in slots], axis=0)[:, 0:1]
    coefs = jnp.concatenate([low, high], axis=1)
    stacked = jnp.concatenate(three(coefs), axis=0)
    parts = lax.dot_general(
        stacked, x_ref[...], (((1,), (1,)), ((), ())), preferred_element_type=F32
    )
    per_leaf = (
        parts[:LEAVES] + (parts[LEAVES : 2 * LEAVES] + parts[2 * LEAVES :])
    ) + shift
    leaf_all = lanes_of(table[4])
    leaf_at = (iota(per_leaf.shape, 0) ^ slot_mask(position())).astype(F32)
    chosen = jnp.sum(jnp.where(leaf_all == leaf_at, per_leaf, 0.0), axis=0, keepdims=True)
    for b in range(tree_ref.shape[0]):
        piece = chosen[:, b * LANE : (b + 1) * LANE]
        tree_ref[b : b + 1, :] = piece
        new_ref[b : b + 1, :] = table[3, b : b + 1, :] + SHRINKAGE * piece


def row_outputs(table, x, coefs):
    row = (table.shape[1:], F32)
    return on_chip(output_kernel, (row, row), [], (table, x, *coefs))


def body(features, scores, labels, query_ids, ranks, leaf_ids):
    devices = lax.axis_size("doc") * lax.axis_size("leaf")
    n_rows = features.shape[0]
    score, label, query, rank, leaf = [
        v.reshape(n_rows // LANE, LANE) for v in (scores, labels, query_ids, ranks, leaf_ids)
    ]

    def swapped(value, flip):
        return lax.ppermute(value, AXES, [(i, i ^ flip) for i in range(devices)])

    x = features
    inner, outer, table = edges(query, label, rank, score, leaf)
    inner = swapped(inner, 1)
    outer = lax.ppermute(
        outer, AXES, [p for i in range(1, devices - 1, 2) for p in ((i, i + 1), (i + 1, i))]
    )
    grad, hess = interior(table)
    grad, send, *sums, held = boundary(table, x, inner, outer, grad, hess)
    chunks = []
    for codes in NEAR:
        if chunks:
            send = gram_part(other_core(codes), table, held, *sums)
        other = swapped(send, 1)
        folded = fold(gram_part(codes, table, held, *sums), other)
        chunks += [swapped(c, 2 * code) if code else c for c, code in zip(folded, codes)]
    mine = total(chunks)
    parts = [mine, swapped(mine, 16)]
    bit = 32
    while bit < devices:
        mine = parts[0] + parts[1]
        parts = [mine, swapped(mine, bit)]
        bit *= 2
    coefs = solve_leaf(parts)
    group = jnp.stack([swapped(coefs, flip) if flip else coefs for flip in GATHER[0]])
    coefs = [swapped(group, flip) if flip else group for flip in GATHER[1]]
    tree, fresh = row_outputs(table, x, coefs)
    return grad.reshape(-1), tree.reshape(-1), fresh.reshape(-1)


def solution(mesh):
    rows = P(AXES)
    return jax.shard_map(
        body,
        mesh=mesh,
        in_specs=(P(AXES, None), rows, rows, rows, rows, rows),
        out_specs=(rows, rows, rows),
        check_vma=False,
    )
```

```python
import functools

import jax
import jax.numpy as jnp
import numpy as np
from jax import lax
from jax.experimental import pallas as pl
from jax.experimental.pallas import tpu as pltpu
from jax.sharding import PartitionSpec as P

LEAVES = 16
MAXQ = 128
LAMBDA = 1.0
SHRINKAGE = 0.1
AXES = ("doc", "leaf")
LANE = 128
EXTRA = 8
STRIP = 32
GROUP = 16
NEAR = ((0, 4, 2, 1), (7, 6, 5, 3))
PART = 4
VMEM_LIMIT = 48 * 1024 * 1024
F32 = jnp.float32
BF16 = jnp.bfloat16


def iota(shape, dim):
    return lax.broadcasted_iota(jnp.int32, shape, dim)


def lanes_of(block_rows):
    return jnp.concatenate(
        [block_rows[b : b + 1, :] for b in range(block_rows.shape[0])], axis=1
    )


def position():
    return lax.axis_index("doc") * lax.axis_size("leaf") + lax.axis_index("leaf")


def slot_mask(me):
    return (me & 1) * 8 + ((me >> 2) & 3) * 2 + ((me >> 1) & 1)


def other_core(codes):
    return tuple(code + LEAVES // 2 for code in codes)


def fetch(sources, places, sems):
    copies = [
        pltpu.make_async_copy(src, dst, sems.at[n])
        for n, (src, dst) in enumerate(zip(sources, places))
    ]
    for copy in copies:
        copy.start()
    return copies


def edge_kernel(
    query_hbm, label_hbm, rank_hbm, score_hbm, leaf_hbm,
    inner_ref, outer_ref, table_ref, query, label, rank, score, leaf, sems,
):
    odd = (position() & 1) == 1
    copies = fetch(
        (query_hbm, label_hbm, rank_hbm, score_hbm, leaf_hbm),
        (query, label, rank, score, leaf),
        sems,
    )
    blocks = query.shape[0]
    for copy in copies:
        copy.wait()
    for n, ref in enumerate((query, label, rank, score, leaf)):
        value = ref[...].astype(F32)
        table_ref[n] = value
        if n < 4:
            first, last = value[0:1, :], value[blocks - 1 : blocks, :]
            inner_ref[n : n + 1, :] = jnp.where(odd, first, last)
            outer_ref[n : n + 1, :] = jnp.where(odd, last, first)


def edges(query, label, rank, score, leaf):
    blocks = score.shape[0]
    anywhere = pl.BlockSpec(memory_space=pltpu.HBM)
    vmem = pl.BlockSpec(memory_space=pltpu.VMEM)
    edge = jax.ShapeDtypeStruct((4, LANE), F32)
    whole = pltpu.VMEM((blocks, LANE), jnp.int32)
    return pl.pallas_call(
        edge_kernel,
        out_shape=(edge, edge, jax.ShapeDtypeStruct((5, blocks, LANE), F32)),
        in_specs=[anywhere] * 5,
        out_specs=(vmem,) * 3,
        scratch_shapes=[whole, whole, whole, pltpu.VMEM((blocks, LANE), F32), whole]
        + [pltpu.SemaphoreType.DMA((5,))],
    )(query, label, rank, score, leaf)


def pair_tables(query, label, rank, score, rows, cols, packed_cols):
    count = query.shape[0]
    gain = jnp.exp2(label)
    disc = 1.0 / jnp.log2(1.0 + jnp.maximum(rank, 1.0))
    expo = jnp.exp(score)
    for slot, value in enumerate((query, gain, disc, expo)):
        rows[slot, 0:count, :] = value
        turned = value.T
        for b in range(count):
            cols[slot, b * LANE : (b + 1) * LANE, :] = jnp.broadcast_to(
                turned[:, b : b + 1], (LANE, LANE)
            )
    grade = label.T
    turned = (
        jnp.where(grade >= 1.0, 1, 0)
        + jnp.where(grade >= 2.0, 1 << 8, 0)
        + jnp.where(grade >= 3.0, 1 << 16, 0)
        + jnp.where(grade >= 4.0, 1 << 24, 0)
    )
    for b in range(count):
        packed_cols[b * LANE : (b + 1) * LANE, :] = jnp.broadcast_to(
            turned[:, b : b + 1], (LANE, LANE)
        )


def rank_table():
    positions = iota((LANE, LANE), 0).astype(F32) + 1.0
    return positions, 1.0 / jnp.log2(1.0 + positions)


def pair_block(own, start, rows, cols, packed_cols, ranked):
    positions, position_disc = ranked
    own_q = rows[0, pl.ds(own, 1), :]
    own_g = rows[1, pl.ds(own, 1), :]
    own_d = rows[2, pl.ds(own, 1), :]
    own_e = rows[3, pl.ds(own, 1), :]
    grad_sum = jnp.zeros((8, LANE), F32)
    hess_sum = jnp.zeros((8, LANE), F32)
    counts = jnp.zeros((8, LANE), jnp.int32)
    for chunk in range(3 * LANE // 8):
        at = pl.ds(pl.multiple_of(start * LANE + chunk * 8, 8), 8)
        far_e = cols[3, at, :]
        same = cols[0, at, :] == own_q
        gap = own_g - cols[1, at, :]
        signed = jnp.where(same, gap * jnp.abs(own_d - cols[2, at, :]), 0.0)
        inv = 1.0 / (own_e + far_e)
        scaled = signed * inv
        grad_sum = grad_sum + scaled * jnp.where(gap > 0.0, far_e, own_e)
        hess_sum = hess_sum + jnp.abs(scaled) * (far_e * inv)
        counts = counts + jnp.where(same, packed_cols[at, :], 0)
    count = jnp.sum(counts, axis=0, keepdims=True)
    grad = jnp.sum(grad_sum, axis=0, keepdims=True)
    hess = jnp.sum(hess_sum, axis=0, keepdims=True) * own_e
    ideal = jnp.zeros((LANE, LANE), F32)
    for k in range(4):
        count_k = (lax.shift_right_logical(count, 8 * k) & 255).astype(F32)
        ideal = ideal + jnp.where(positions <= count_k, float(1 << k), 0.0)
    ideal = jnp.sum(ideal * position_disc, axis=0, keepdims=True)
    norm = 1.0 / jnp.maximum(ideal, 1.0)
    return -norm * grad, norm * hess


def leaf_sums(x, turned, hess_all, grad_all, leaf_all, weighted, moment_s, hsum_s, total_s):
    n_rows = leaf_all.shape[1]
    weighted[...] = (turned * hess_all).astype(BF16)
    member = leaf_all == iota((LEAVES, n_rows), 0)
    member_low = jnp.where(member, 1.0, 0.0).astype(BF16)
    grad_low = jnp.where(member, grad_all, 0.0).astype(BF16)
    moment_s[...] = jnp.dot(grad_low, x, preferred_element_type=F32)
    hsum_s[...] = lax.dot_general(
        member_low, weighted[...], (((1,), (1,)), ((), ())), preferred_element_type=F32
    )
    htot = jnp.sum(jnp.where(member, hess_all, 0.0), axis=1, keepdims=True)
    gtot = jnp.sum(jnp.where(member, grad_all, 0.0), axis=1, keepdims=True)
    lane_at = iota((LEAVES, LANE), 1)
    total_s[...] = jnp.where(lane_at == 0, htot, jnp.where(lane_at == 1, gtot, 0.0))


def pack_grams(x_ref, leaf_all, weighted, moment_s, hsum_s, total_s, out_ref, codes):
    half = x_ref.shape[1] // 2
    mask = slot_mask(position())
    down = iota((half, half), 0)
    across = iota((half, half), 1)

    for slot, code in enumerate(codes):
        leaf = mask ^ code
        chosen = jnp.where(leaf_all == leaf.astype(F32), 1.0, 0.0).astype(BF16)
        gram = jnp.dot(weighted[...] * chosen, x_ref[...], preferred_element_type=F32)
        out_ref[slot, 0:half, :] = gram[half:, :half]
        out_ref[slot, half : 2 * half, :] = jnp.where(
            down >= across, gram[:half, :half], gram[half:, half:]
        )
        diagonal = jnp.sum(
            jnp.where(down == across, gram[half:, half:], 0.0), axis=0, keepdims=True
        )
        hs = hsum_s[pl.ds(leaf, 1), :]
        mo = moment_s[pl.ds(leaf, 1), :]
        to = total_s[pl.ds(leaf, 1), :]
        out_ref[slot, 2 * half :, :] = jnp.concatenate(
            [diagonal, hs[:, :half], hs[:, half:], mo[:, :half], mo[:, half:], to]
            + [jnp.zeros((EXTRA - 6, LANE), F32)],
            axis=0,
        )


def interior_kernel(table, grad_ref, hess_ref, rows, cols, packed_cols):
    blocks = grad_ref.shape[0]
    pair_tables(table[0], table[1], table[2], table[3], rows, cols, packed_cols)
    nothing = jnp.zeros((1, LANE), F32)
    for ref in (grad_ref, hess_ref):
        ref[0:1, :] = nothing
        ref[blocks - 1 : blocks, :] = nothing

    ranked = rank_table()

    def one_block(b, carry):
        grad, hess = pair_block(b, b - 1, rows, cols, packed_cols, ranked)
        grad_ref[pl.ds(b, 1), :] = grad
        hess_ref[pl.ds(b, 1), :] = hess
        return carry

    lax.fori_loop(1, blocks - 1, one_block, 0, unroll=6)


def boundary_kernel(
    table, x_ref, inner, outer, grad_part, hess_part,
    grad_ref, send_ref, weighted, moment_s, hsum_s, total_s, x_out,
    rows, cols, packed_cols,
):
    blocks = grad_ref.shape[0]
    final = blocks - 1
    me = position()
    devices = lax.axis_size("doc") * lax.axis_size("leaf")

    odd = (me & 1) == 1

    def window(slot):
        near = inner[slot : slot + 1, :]
        far = outer[slot : slot + 1, :]
        return jnp.concatenate(
            [
                jnp.where(odd, near, far),
                table[slot, 0:2, :],
                table[slot, final - 1 :, :],
                jnp.where(odd, far, near),
            ],
            axis=0,
        )

    ids = window(0)
    at = iota(ids.shape, 0)
    outside = ((at == 0) & (me == 0)) | ((at == 5) & (me == devices - 1))
    pair_tables(
        jnp.where(outside, -1.0, ids), window(1), window(2), window(3), rows, cols, packed_cols
    )
    ranked = rank_table()
    head_grad, head_hess = pair_block(1, 0, rows, cols, packed_cols, ranked)
    tail_grad, tail_hess = pair_block(4, 3, rows, cols, packed_cols, ranked)
    grads = jnp.concatenate([head_grad, grad_part[1:final, :], tail_grad], axis=0)
    hesses = jnp.concatenate([head_hess, hess_part[1:final, :], tail_hess], axis=0)
    grad_ref[...] = grads
    x_out[...] = x_ref[...]
    leaf_all = lanes_of(table[4])
    leaf_sums(
        x_ref[...], x_ref[...].astype(F32).T, lanes_of(hesses), lanes_of(grads), leaf_all,
        weighted, moment_s, hsum_s, total_s,
    )
    pack_grams(x_ref, leaf_all, weighted, moment_s, hsum_s, total_s, send_ref, other_core(NEAR[0]))


def gram_kernel(codes, table, x_ref, weighted, moment_s, hsum_s, total_s, out_ref):
    pack_grams(
        x_ref, lanes_of(table[4]), weighted, moment_s, hsum_s, total_s, out_ref, codes
    )


def table_scratch(count):
    return [
        pltpu.VMEM((4, 8 * pl.cdiv(count, 8), LANE), F32),
        pltpu.VMEM((4, count * LANE, LANE), F32),
        pltpu.VMEM((count * LANE, LANE), jnp.int32),
    ]


def on_chip(kernel, outs, scratch, args, cost=None):
    vmem = pl.BlockSpec(memory_space=pltpu.VMEM)
    return pl.pallas_call(
        kernel,
        out_shape=tuple(jax.ShapeDtypeStruct(shape, kind) for shape, kind in outs),
        in_specs=[vmem] * len(args),
        out_specs=(vmem,) * len(outs),
        scratch_shapes=scratch,
        compiler_params=pltpu.CompilerParams(vmem_limit_bytes=VMEM_LIMIT),
        cost_estimate=cost,
    )(*args)


def interior(table):
    _, blocks, _ = table.shape
    cost = pl.CostEstimate(
        flops=20000 * blocks * LANE * LANE, bytes_accessed=blocks * LANE * LANE, transcendentals=0
    )
    row = ((blocks, LANE), F32)
    return on_chip(interior_kernel, (row, row), table_scratch(blocks), (table,), cost)


def boundary(table, x, inner, outer, grad, hess):
    n_rows, feats = x.shape
    outs = (
        (grad.shape, F32),
        ((PART, feats + EXTRA, LANE), F32),
        ((feats, n_rows), BF16),
        ((LEAVES, feats), F32),
        ((LEAVES, feats), F32),
        ((LEAVES, LANE), F32),
        (x.shape, x.dtype),
    )
    return on_chip(
        boundary_kernel, outs, table_scratch(6), (table, x, inner, outer, grad, hess)
    )


def gram_part(codes, table, x, weighted, moment, hsum, totals):
    n_rows, feats = x.shape
    cost = pl.CostEstimate(
        flops=8 * PART * n_rows * feats * feats, bytes_accessed=n_rows * feats, transcendentals=0
    )
    outs = (((PART, feats + EXTRA, LANE), F32),)
    kernel = functools.partial(gram_kernel, codes)
    return on_chip(kernel, outs, [], (table, x, weighted, moment, hsum, totals), cost)[0]


def fold_kernel(keep_ref, other_ref, *outs):
    for n, out in enumerate(outs):
        out[...] = keep_ref[n] + other_ref[n]


def fold(keep, other):
    return on_chip(fold_kernel, ((keep.shape[1:], F32),) * keep.shape[0], [], (keep, other))


def tree_sum(values):
    while len(values) > 1:
        values = [a + b for a, b in zip(values[::2], values[1::2])]
    return values[0]


def total_kernel(*refs):
    refs[-1][...] = tree_sum([ref[...] for ref in refs[:-1]])


def total(parts):
    return on_chip(total_kernel, ((parts[0].shape, F32),), [], parts)[0]


def eliminate(tiles, at, offset):
    size = tiles[at].shape[0]
    down = iota((size, LANE), 0)
    scale = jnp.ones((size, LANE), F32)
    for base in range(0, size, GROUP):
        first = offset + base
        columns = [
            jnp.broadcast_to(tiles[at][:, first + j : first + j + 1], (size, LANE))
            for j in range(GROUP)
        ]
        for j in range(GROUP):
            p = base + j
            inverse = 1.0 / columns[j][p : p + 1, :]
            scale = jnp.where(down == p, inverse, scale)
            factor = jnp.where(down == p, 0.0, columns[j]) * inverse
            for k in range(j + 1, GROUP):
                columns[k] = columns[k] - factor * columns[k][p : p + 1, :]
            tiles = [t if t is None else t - factor * t[p : p + 1, :] for t in tiles]
    return [t if t is None else t * scale for t in tiles]


def three(value):
    top = value.astype(BF16)
    left = value - top.astype(F32)
    middle = left.astype(BF16)
    return top, middle, (left - middle.astype(F32)).astype(BF16)


def left_parts(value):
    top, middle, bottom = three(value)
    return jnp.concatenate([top, top, middle, top, middle, bottom], axis=1)


def right_parts(value):
    top, middle, bottom = three(value)
    return jnp.concatenate([top, middle, top, bottom, middle, top], axis=0)


def solve_kernel(*refs):
    ins, out_ref = refs[:-1], refs[-1]
    summed = tree_sum([ref[...] for ref in ins])
    feats = summed.shape[0] - EXTRA
    half = feats // 2
    corner = summed[:half]
    mixed = summed[half:feats]
    extra = [summed[feats + n : feats + n + 1] for n in range(6)]
    turned = mixed.T
    down = iota((half, half), 0)
    across = iota((half, half), 1)
    diag_row, hs0, hs1, mo0, mo1, totals = extra
    upper_left = jnp.where(down >= across, mixed, turned)
    lower_right = jnp.where(down < across, mixed, jnp.where(down > across, turned, diag_row))
    htot = totals[:, 0:1]
    gtot = totals[:, 1:2]
    inv_den = 1.0 / (htot + LAMBDA)
    rhs0 = hs0 * (gtot * inv_den) - mo0
    rhs1 = hs1 * (gtot * inv_den) - mo1
    columns = jnp.concatenate(
        [hs0, hs1, rhs0, rhs1, jnp.zeros((4, LANE), F32)], axis=0
    ).T
    hc0 = columns[:, 0:1] * inv_den
    hc1 = columns[:, 1:2] * inv_den
    eye = jnp.where(down == across, LAMBDA, 0.0)
    top = [
        upper_left + eye - hc0 * hs0,
        corner.T - hc0 * hs1,
        jnp.where(across == 0, columns[:, 2:3], 0.0),
    ]
    low = [
        corner - hc1 * hs0,
        lower_right + eye - hc1 * hs1,
        jnp.where(across == 0, columns[:, 3:4], 0.0),
    ]
    per_tile = LANE // STRIP
    count = feats // STRIP
    strips = []
    for s in range(count):
        source = top if s < per_tile else low
        start = (s % per_tile) * STRIP
        strips.append([t[start : start + STRIP] for t in source])
    for s in range(count):
        tile, offset = s // per_tile, (s % per_tile) * STRIP
        done = eliminate([None] * tile + strips[s][tile:], tile, offset)
        strips[s] = done
        solved = right_parts(jnp.concatenate(done[tile:], axis=1))
        later = [s + 1] if s + 1 < count else []
        others = [i for i in range(count) if i not in (s, s + 1)]
        for group in (later, others):
            if not group:
                continue
            left = jnp.concatenate(
                [strips[i][tile][:, offset : offset + STRIP] for i in group], axis=0
            )
            change = jnp.dot(left_parts(left), solved, preferred_element_type=F32)
            for q, i in enumerate(group):
                part = change[q * STRIP : (q + 1) * STRIP]
                strips[i] = [
                    t if n < tile else t - part[:, (n - tile) * LANE : (n - tile + 1) * LANE]
                    for n, t in enumerate(strips[i])
                ]
    right = [strips[s][2] for s in range(count)]
    w0 = jnp.concatenate(right[:per_tile], axis=0).T[0:1, :]
    w1 = jnp.concatenate(right[per_tile:], axis=0).T[0:1, :]
    dotted = jnp.sum(hs0 * w0 + hs1 * w1, axis=1, keepdims=True)
    intercept = -(gtot + dotted) * inv_den
    result = jnp.concatenate(
        [w0, w1, jnp.broadcast_to(intercept, (1, LANE)), jnp.zeros((1, LANE), F32)], axis=0
    )
    out_ref[...] = jnp.broadcast_to(result[None], out_ref.shape)


def solve_leaf(parts, copies):
    return on_chip(solve_kernel, (((copies, 4, LANE), F32),), [], parts)[0]


def output_kernel(table, x_ref, coef_ref, tree_ref, new_ref):
    slots = [coef_ref[(n >> 3) * 17 + (n & 7) * 2] for n in range(LEAVES)]
    low = jnp.concatenate([c[0:1, :] for c in slots], axis=0)
    high = jnp.concatenate([c[1:2, :] for c in slots], axis=0)
    shift = jnp.concatenate([c[2:3, :] for c in slots], axis=0)[:, 0:1]
    coefs = jnp.concatenate([low, high], axis=1)
    stacked = jnp.concatenate(three(coefs), axis=0)
    parts = lax.dot_general(
        stacked, x_ref[...], (((1,), (1,)), ((), ())), preferred_element_type=F32
    )
    per_leaf = (
        parts[:LEAVES] + (parts[LEAVES : 2 * LEAVES] + parts[2 * LEAVES :])
    ) + shift
    leaf_all = lanes_of(table[4])
    leaf_at = iota(per_leaf.shape, 0).astype(F32)
    chosen = jnp.sum(jnp.where(leaf_all == leaf_at, per_leaf, 0.0), axis=0, keepdims=True)
    for b in range(tree_ref.shape[0]):
        piece = chosen[:, b * LANE : (b + 1) * LANE]
        tree_ref[b : b + 1, :] = piece
        new_ref[b : b + 1, :] = table[3, b : b + 1, :] + SHRINKAGE * piece


def row_outputs(table, x, coefs):
    row = (table.shape[1:], F32)
    return on_chip(output_kernel, (row, row), [], (table, x, coefs))


def body(features, scores, labels, query_ids, ranks, leaf_ids):
    devices = lax.axis_size("doc") * lax.axis_size("leaf")
    n_rows = features.shape[0]
    score, label, query, rank, leaf = [
        v.reshape(n_rows // LANE, LANE) for v in (scores, labels, query_ids, ranks, leaf_ids)
    ]

    def swapped(value, flip):
        return lax.ppermute(value, AXES, [(i, i ^ flip) for i in range(devices)])

    x = features
    inner, outer, table = edges(query, label, rank, score, leaf)
    inner = swapped(inner, 1)
    outer = lax.ppermute(
        outer, AXES, [p for i in range(1, devices - 1, 2) for p in ((i, i + 1), (i + 1, i))]
    )
    grad, hess = interior(table)
    grad, send, *sums, held = boundary(table, x, inner, outer, grad, hess)
    chunks = []
    for codes in NEAR:
        if chunks:
            send = gram_part(other_core(codes), table, held, *sums)
        other = swapped(send, 1)
        folded = fold(gram_part(codes, table, held, *sums), other)
        chunks += [swapped(c, 2 * code) if code else c for c, code in zip(folded, codes)]
    mine = total(chunks)
    owner = [(d >> 4 & 1) == (d & 1) for d in range(devices)]
    parts = [mine, lax.ppermute(mine, AXES, [(d, d ^ (1 if o else 16)) for d, o in enumerate(owner)])]
    bit = 32
    while bit < devices:
        mine = parts[0] + parts[1]
        parts = [mine, swapped(mine, bit)]
        bit *= 2
    coefs = lax.all_to_all(solve_leaf(parts, devices), AXES, 0, 0, tiled=True)
    tree, fresh = row_outputs(table, x, coefs)
    return grad.reshape(-1), tree.reshape(-1), fresh.reshape(-1)


def solution(mesh):
    rows = P(AXES)
    return jax.shard_map(
        body,
        mesh=mesh,
        in_specs=(P(AXES, None), rows, rows, rows, rows, rows),
        out_specs=(rows, rows, rows),
        check_vma=False,
    )
```

```python
import functools

import jax
import jax.numpy as jnp
import numpy as np
from jax import lax
from jax.experimental import pallas as pl
from jax.experimental.pallas import tpu as pltpu
from jax.sharding import PartitionSpec as P

LEAVES = 16
MAXQ = 128
LAMBDA = 1.0
SHRINKAGE = 0.1
AXES = ("doc", "leaf")
LANE = 128
EXTRA = 8
STRIP = 32
GROUP = 16
NEAR = ((0, 4, 2, 1), (7, 6, 5, 3))
PART = 4
VMEM_LIMIT = 32 * 1024 * 1024
F32 = jnp.float32
BF16 = jnp.bfloat16


def iota(shape, dim):
    return lax.broadcasted_iota(jnp.int32, shape, dim)


def lanes_of(block_rows):
    return jnp.concatenate(
        [block_rows[b : b + 1, :] for b in range(block_rows.shape[0])], axis=1
    )


def position():
    return lax.axis_index("doc") * lax.axis_size("leaf") + lax.axis_index("leaf")


def slot_mask(me):
    return (me & 1) * 8 + ((me >> 2) & 3) * 2 + ((me >> 1) & 1)


def other_core(codes):
    return tuple(code + LEAVES // 2 for code in codes)


def fetch(sources, places, sems):
    copies = [
        pltpu.make_async_copy(src, dst, sems.at[n])
        for n, (src, dst) in enumerate(zip(sources, places))
    ]
    for copy in copies:
        copy.start()
    return copies


def edge_kernel(
    query_hbm, label_hbm, rank_hbm, score_hbm, leaf_hbm,
    inner_ref, outer_ref, table_ref, query, label, rank, score, leaf, sems,
):
    odd = (position() & 1) == 1
    copies = fetch(
        (query_hbm, label_hbm, rank_hbm, score_hbm, leaf_hbm),
        (query, label, rank, score, leaf),
        sems,
    )
    blocks = query.shape[0]
    for copy in copies:
        copy.wait()
    for n, ref in enumerate((query, label, rank, score, leaf)):
        value = ref[...].astype(F32)
        table_ref[n] = value
        if n < 4:
            first, last = value[0:1, :], value[blocks - 1 : blocks, :]
            inner_ref[n : n + 1, :] = jnp.where(odd, first, last)
            outer_ref[n : n + 1, :] = jnp.where(odd, last, first)


def edges(query, label, rank, score, leaf):
    blocks = score.shape[0]
    anywhere = pl.BlockSpec(memory_space=pltpu.HBM)
    vmem = pl.BlockSpec(memory_space=pltpu.VMEM)
    edge = jax.ShapeDtypeStruct((4, LANE), F32)
    whole = pltpu.VMEM((blocks, LANE), jnp.int32)
    return pl.pallas_call(
        edge_kernel,
        out_shape=(edge, edge, jax.ShapeDtypeStruct((5, blocks, LANE), F32)),
        in_specs=[anywhere] * 5,
        out_specs=(vmem,) * 3,
        scratch_shapes=[whole, whole, whole, pltpu.VMEM((blocks, LANE), F32), whole]
        + [pltpu.SemaphoreType.DMA((5,))],
    )(query, label, rank, score, leaf)


def pair_tables(query, label, rank, score, rows, cols, packed_cols):
    count = query.shape[0]
    gain = jnp.exp2(label)
    disc = 1.0 / jnp.log2(1.0 + jnp.maximum(rank, 1.0))
    expo = jnp.exp(score)
    for slot, value in enumerate((query, gain, disc, expo)):
        rows[slot, 0:count, :] = value
        turned = value.T
        for b in range(count):
            cols[slot, b * LANE : (b + 1) * LANE, :] = jnp.broadcast_to(
                turned[:, b : b + 1], (LANE, LANE)
            )
    grade = label.T
    turned = (
        jnp.where(grade >= 1.0, 1, 0)
        + jnp.where(grade >= 2.0, 1 << 8, 0)
        + jnp.where(grade >= 3.0, 1 << 16, 0)
        + jnp.where(grade >= 4.0, 1 << 24, 0)
    )
    for b in range(count):
        packed_cols[b * LANE : (b + 1) * LANE, :] = jnp.broadcast_to(
            turned[:, b : b + 1], (LANE, LANE)
        )


def rank_table():
    positions = iota((LANE, LANE), 0).astype(F32) + 1.0
    return positions, 1.0 / jnp.log2(1.0 + positions)


def pair_block(own, start, rows, cols, packed_cols, ranked):
    positions, position_disc = ranked
    own_q = rows[0, pl.ds(own, 1), :]
    own_g = rows[1, pl.ds(own, 1), :]
    own_d = rows[2, pl.ds(own, 1), :]
    own_e = rows[3, pl.ds(own, 1), :]
    grad_sum = jnp.zeros((8, LANE), F32)
    hess_sum = jnp.zeros((8, LANE), F32)
    counts = jnp.zeros((8, LANE), jnp.int32)
    for chunk in range(3 * LANE // 8):
        at = pl.ds(pl.multiple_of(start * LANE + chunk * 8, 8), 8)
        far_e = cols[3, at, :]
        same = cols[0, at, :] == own_q
        gap = own_g - cols[1, at, :]
        signed = jnp.where(same, gap * jnp.abs(own_d - cols[2, at, :]), 0.0)
        inv = 1.0 / (own_e + far_e)
        scaled = signed * inv
        grad_sum = grad_sum + scaled * jnp.where(gap > 0.0, far_e, own_e)
        hess_sum = hess_sum + jnp.abs(scaled) * (far_e * inv)
        counts = counts + jnp.where(same, packed_cols[at, :], 0)
    count = jnp.sum(counts, axis=0, keepdims=True)
    grad = jnp.sum(grad_sum, axis=0, keepdims=True)
    hess = jnp.sum(hess_sum, axis=0, keepdims=True) * own_e
    ideal = jnp.zeros((LANE, LANE), F32)
    for k in range(4):
        count_k = (lax.shift_right_logical(count, 8 * k) & 255).astype(F32)
        ideal = ideal + jnp.where(positions <= count_k, float(1 << k), 0.0)
    ideal = jnp.sum(ideal * position_disc, axis=0, keepdims=True)
    norm = 1.0 / jnp.maximum(ideal, 1.0)
    return -norm * grad, norm * hess


def leaf_sums(x, turned, hess_all, grad_all, leaf_all, weighted, moment_s, hsum_s, total_s):
    n_rows = leaf_all.shape[1]
    weighted[...] = (turned * hess_all).astype(BF16)
    member = leaf_all == iota((LEAVES, n_rows), 0)
    member_low = jnp.where(member, 1.0, 0.0).astype(BF16)
    grad_low = jnp.where(member, grad_all, 0.0).astype(BF16)
    moment_s[...] = jnp.dot(grad_low, x, preferred_element_type=F32)
    hsum_s[...] = lax.dot_general(
        member_low, weighted[...], (((1,), (1,)), ((), ())), preferred_element_type=F32
    )
    htot = jnp.sum(jnp.where(member, hess_all, 0.0), axis=1, keepdims=True)
    gtot = jnp.sum(jnp.where(member, grad_all, 0.0), axis=1, keepdims=True)
    lane_at = iota((LEAVES, LANE), 1)
    total_s[...] = jnp.where(lane_at == 0, htot, jnp.where(lane_at == 1, gtot, 0.0))


def pack_grams(x_ref, leaf_all, weighted, moment_s, hsum_s, total_s, out_ref, codes):
    half = x_ref.shape[1] // 2
    mask = slot_mask(position())
    down = iota((half, half), 0)
    across = iota((half, half), 1)

    for slot, code in enumerate(codes):
        leaf = mask ^ code
        chosen = jnp.where(leaf_all == leaf.astype(F32), 1.0, 0.0).astype(BF16)
        gram = jnp.dot(weighted[...] * chosen, x_ref[...], preferred_element_type=F32)
        out_ref[slot, 0:half, :] = gram[half:, :half]
        out_ref[slot, half : 2 * half, :] = jnp.where(
            down >= across, gram[:half, :half], gram[half:, half:]
        )
        diagonal = jnp.sum(
            jnp.where(down == across, gram[half:, half:], 0.0), axis=0, keepdims=True
        )
        hs = hsum_s[pl.ds(leaf, 1), :]
        mo = moment_s[pl.ds(leaf, 1), :]
        to = total_s[pl.ds(leaf, 1), :]
        out_ref[slot, 2 * half :, :] = jnp.concatenate(
            [diagonal, hs[:, :half], hs[:, half:], mo[:, :half], mo[:, half:], to]
            + [jnp.zeros((EXTRA - 6, LANE), F32)],
            axis=0,
        )


def interior_kernel(table, grad_ref, hess_ref, rows, cols, packed_cols):
    blocks = grad_ref.shape[0]
    pair_tables(table[0], table[1], table[2], table[3], rows, cols, packed_cols)
    nothing = jnp.zeros((1, LANE), F32)
    for ref in (grad_ref, hess_ref):
        ref[0:1, :] = nothing
        ref[blocks - 1 : blocks, :] = nothing

    ranked = rank_table()

    def one_block(b, carry):
        grad, hess = pair_block(b, b - 1, rows, cols, packed_cols, ranked)
        grad_ref[pl.ds(b, 1), :] = grad
        hess_ref[pl.ds(b, 1), :] = hess
        return carry

    lax.fori_loop(1, blocks - 1, one_block, 0, unroll=6)


def boundary_kernel(
    table, x_ref, inner, outer, grad_part, hess_part,
    grad_ref, send_ref, weighted, moment_s, hsum_s, total_s, x_out,
    rows, cols, packed_cols,
):
    blocks = grad_ref.shape[0]
    final = blocks - 1
    me = position()
    devices = lax.axis_size("doc") * lax.axis_size("leaf")

    odd = (me & 1) == 1

    def window(slot):
        near = inner[slot : slot + 1, :]
        far = outer[slot : slot + 1, :]
        return jnp.concatenate(
            [
                jnp.where(odd, near, far),
                table[slot, 0:2, :],
                table[slot, final - 1 :, :],
                jnp.where(odd, far, near),
            ],
            axis=0,
        )

    ids = window(0)
    at = iota(ids.shape, 0)
    outside = ((at == 0) & (me == 0)) | ((at == 5) & (me == devices - 1))
    pair_tables(
        jnp.where(outside, -1.0, ids), window(1), window(2), window(3), rows, cols, packed_cols
    )
    ranked = rank_table()
    head_grad, head_hess = pair_block(1, 0, rows, cols, packed_cols, ranked)
    tail_grad, tail_hess = pair_block(4, 3, rows, cols, packed_cols, ranked)
    grads = jnp.concatenate([head_grad, grad_part[1:final, :], tail_grad], axis=0)
    hesses = jnp.concatenate([head_hess, hess_part[1:final, :], tail_hess], axis=0)
    grad_ref[...] = grads
    x_out[...] = x_ref[...]
    leaf_all = lanes_of(table[4])
    leaf_sums(
        x_ref[...], x_ref[...].astype(F32).T, lanes_of(hesses), lanes_of(grads), leaf_all,
        weighted, moment_s, hsum_s, total_s,
    )
    pack_grams(x_ref, leaf_all, weighted, moment_s, hsum_s, total_s, send_ref, other_core(NEAR[0]))


def gram_kernel(codes, table, x_ref, weighted, moment_s, hsum_s, total_s, out_ref):
    pack_grams(
        x_ref, lanes_of(table[4]), weighted, moment_s, hsum_s, total_s, out_ref, codes
    )


def table_scratch(count):
    return [
        pltpu.VMEM((4, 8 * pl.cdiv(count, 8), LANE), F32),
        pltpu.VMEM((4, count * LANE, LANE), F32),
        pltpu.VMEM((count * LANE, LANE), jnp.int32),
    ]


def on_chip(kernel, outs, scratch, args, cost=None):
    vmem = pl.BlockSpec(memory_space=pltpu.VMEM)
    return pl.pallas_call(
        kernel,
        out_shape=tuple(jax.ShapeDtypeStruct(shape, kind) for shape, kind in outs),
        in_specs=[vmem] * len(args),
        out_specs=(vmem,) * len(outs),
        scratch_shapes=scratch,
        compiler_params=pltpu.CompilerParams(vmem_limit_bytes=VMEM_LIMIT),
        cost_estimate=cost,
    )(*args)


def interior(table):
    _, blocks, _ = table.shape
    cost = pl.CostEstimate(
        flops=20000 * blocks * LANE * LANE, bytes_accessed=blocks * LANE * LANE, transcendentals=0
    )
    row = ((blocks, LANE), F32)
    return on_chip(interior_kernel, (row, row), table_scratch(blocks), (table,), cost)


def boundary(table, x, inner, outer, grad, hess):
    n_rows, feats = x.shape
    outs = (
        (grad.shape, F32),
        ((PART, feats + EXTRA, LANE), F32),
        ((feats, n_rows), BF16),
        ((LEAVES, feats), F32),
        ((LEAVES, feats), F32),
        ((LEAVES, LANE), F32),
        (x.shape, x.dtype),
    )
    return on_chip(
        boundary_kernel, outs, table_scratch(6), (table, x, inner, outer, grad, hess)
    )


def gram_part(codes, table, x, weighted, moment, hsum, totals):
    n_rows, feats = x.shape
    cost = pl.CostEstimate(
        flops=8 * PART * n_rows * feats * feats, bytes_accessed=n_rows * feats, transcendentals=0
    )
    outs = (((PART, feats + EXTRA, LANE), F32),)
    kernel = functools.partial(gram_kernel, codes)
    return on_chip(kernel, outs, [], (table, x, weighted, moment, hsum, totals), cost)[0]


def fold_kernel(keep_ref, other_ref, *outs):
    for n, out in enumerate(outs):
        out[...] = keep_ref[n] + other_ref[n]


def fold(keep, other):
    return on_chip(fold_kernel, ((keep.shape[1:], F32),) * keep.shape[0], [], (keep, other))


def tree_sum(values):
    while len(values) > 1:
        values = [a + b for a, b in zip(values[::2], values[1::2])]
    return values[0]


def total_kernel(*refs):
    refs[-1][...] = tree_sum([ref[...] for ref in refs[:-1]])


def total(parts):
    return on_chip(total_kernel, ((parts[0].shape, F32),), [], parts)[0]


def eliminate(tiles, at, offset):
    size = tiles[at].shape[0]
    down = iota((size, LANE), 0)
    scale = jnp.ones((size, LANE), F32)
    for base in range(0, size, GROUP):
        first = offset + base
        columns = [
            jnp.broadcast_to(tiles[at][:, first + j : first + j + 1], (size, LANE))
            for j in range(GROUP)
        ]
        for j in range(GROUP):
            p = base + j
            inverse = 1.0 / columns[j][p : p + 1, :]
            scale = jnp.where(down == p, inverse, scale)
            factor = jnp.where(down == p, 0.0, columns[j]) * inverse
            for k in range(j + 1, GROUP):
                columns[k] = columns[k] - factor * columns[k][p : p + 1, :]
            tiles = [t if t is None else t - factor * t[p : p + 1, :] for t in tiles]
    return [t if t is None else t * scale for t in tiles]


def three(value):
    top = value.astype(BF16)
    left = value - top.astype(F32)
    middle = left.astype(BF16)
    return top, middle, (left - middle.astype(F32)).astype(BF16)


def left_parts(value):
    top, middle, bottom = three(value)
    return jnp.concatenate([top, top, middle, top, middle, bottom], axis=1)


def right_parts(value):
    top, middle, bottom = three(value)
    return jnp.concatenate([top, middle, top, bottom, middle, top], axis=0)


def solve_kernel(*refs):
    ins, out_ref = refs[:-1], refs[-1]
    summed = tree_sum([ref[...] for ref in ins])
    feats = summed.shape[0] - EXTRA
    half = feats // 2
    corner = summed[:half]
    mixed = summed[half:feats]
    extra = [summed[feats + n : feats + n + 1] for n in range(6)]
    turned = mixed.T
    down = iota((half, half), 0)
    across = iota((half, half), 1)
    diag_row, hs0, hs1, mo0, mo1, totals = extra
    upper_left = jnp.where(down >= across, mixed, turned)
    lower_right = jnp.where(down < across, mixed, jnp.where(down > across, turned, diag_row))
    htot = totals[:, 0:1]
    gtot = totals[:, 1:2]
    inv_den = 1.0 / (htot + LAMBDA)
    rhs0 = hs0 * (gtot * inv_den) - mo0
    rhs1 = hs1 * (gtot * inv_den) - mo1
    columns = jnp.concatenate(
        [hs0, hs1, rhs0, rhs1, jnp.zeros((4, LANE), F32)], axis=0
    ).T
    hc0 = columns[:, 0:1] * inv_den
    hc1 = columns[:, 1:2] * inv_den
    eye = jnp.where(down == across, LAMBDA, 0.0)
    top = [
        upper_left + eye - hc0 * hs0,
        corner.T - hc0 * hs1,
        jnp.where(across == 0, columns[:, 2:3], 0.0),
    ]
    low = [
        corner - hc1 * hs0,
        lower_right + eye - hc1 * hs1,
        jnp.where(across == 0, columns[:, 3:4], 0.0),
    ]
    per_tile = LANE // STRIP
    count = feats // STRIP
    strips = []
    for s in range(count):
        source = top if s < per_tile else low
        start = (s % per_tile) * STRIP
        strips.append([t[start : start + STRIP] for t in source])
    for s in range(count):
        tile, offset = s // per_tile, (s % per_tile) * STRIP
        done = eliminate([None] * tile + strips[s][tile:], tile, offset)
        strips[s] = done
        solved = right_parts(jnp.concatenate(done[tile:], axis=1))
        later = [s + 1] if s + 1 < count else []
        others = [i for i in range(count) if i not in (s, s + 1)]
        for group in (later, others):
            if not group:
                continue
            left = jnp.concatenate(
                [strips[i][tile][:, offset : offset + STRIP] for i in group], axis=0
            )
            change = jnp.dot(left_parts(left), solved, preferred_element_type=F32)
            for q, i in enumerate(group):
                part = change[q * STRIP : (q + 1) * STRIP]
                strips[i] = [
                    t if n < tile else t - part[:, (n - tile) * LANE : (n - tile + 1) * LANE]
                    for n, t in enumerate(strips[i])
                ]
    right = [strips[s][2] for s in range(count)]
    w0 = jnp.concatenate(right[:per_tile], axis=0).T[0:1, :]
    w1 = jnp.concatenate(right[per_tile:], axis=0).T[0:1, :]
    dotted = jnp.sum(hs0 * w0 + hs1 * w1, axis=1, keepdims=True)
    intercept = -(gtot + dotted) * inv_den
    result = jnp.concatenate(
        [w0, w1, jnp.broadcast_to(intercept, (1, LANE)), jnp.zeros((1, LANE), F32)], axis=0
    )
    out_ref[...] = jnp.broadcast_to(result[None], out_ref.shape)


def solve_leaf(parts, copies):
    return on_chip(solve_kernel, (((copies, 4, LANE), F32),), [], parts)[0]


def output_kernel(table, x_ref, coef_ref, tree_ref, new_ref):
    slots = [coef_ref[(n >> 3) * 17 + (n & 7) * 2] for n in range(LEAVES)]
    low = jnp.concatenate([c[0:1, :] for c in slots], axis=0)
    high = jnp.concatenate([c[1:2, :] for c in slots], axis=0)
    shift = jnp.concatenate([c[2:3, :] for c in slots], axis=0)[:, 0:1]
    coefs = jnp.concatenate([low, high], axis=1)
    stacked = jnp.concatenate(three(coefs), axis=0)
    parts = lax.dot_general(
        stacked, x_ref[...], (((1,), (1,)), ((), ())), preferred_element_type=F32
    )
    per_leaf = (
        parts[:LEAVES] + (parts[LEAVES : 2 * LEAVES] + parts[2 * LEAVES :])
    ) + shift
    leaf_all = lanes_of(table[4])
    leaf_at = iota(per_leaf.shape, 0).astype(F32)
    chosen = jnp.sum(jnp.where(leaf_all == leaf_at, per_leaf, 0.0), axis=0, keepdims=True)
    for b in range(tree_ref.shape[0]):
        piece = chosen[:, b * LANE : (b + 1) * LANE]
        tree_ref[b : b + 1, :] = piece
        new_ref[b : b + 1, :] = table[3, b : b + 1, :] + SHRINKAGE * piece


def row_outputs(table, x, coefs):
    row = (table.shape[1:], F32)
    return on_chip(output_kernel, (row, row), [], (table, x, coefs))


def body(features, scores, labels, query_ids, ranks, leaf_ids):
    devices = lax.axis_size("doc") * lax.axis_size("leaf")
    n_rows = features.shape[0]
    score, label, query, rank, leaf = [
        v.reshape(n_rows // LANE, LANE) for v in (scores, labels, query_ids, ranks, leaf_ids)
    ]

    def swapped(value, flip):
        return lax.ppermute(value, AXES, [(i, i ^ flip) for i in range(devices)])

    x = features
    inner, outer, table = edges(query, label, rank, score, leaf)
    inner = swapped(inner, 1)
    outer = lax.ppermute(
        outer, AXES, [(i, (i + (1 if i % 2 else -1)) % devices) for i in range(devices)]
    )
    grad, hess = interior(table)
    grad, send, *sums, held = boundary(table, x, inner, outer, grad, hess)
    chunks = []
    for codes in NEAR:
        if chunks:
            send = gram_part(other_core(codes), table, held, *sums)
        other = swapped(send, 1)
        folded = fold(gram_part(codes, table, held, *sums), other)
        chunks += [swapped(c, 2 * code) if code else c for c, code in zip(folded, codes)]
    mine = total(chunks)
    owner = [(d >> 4 & 1) == (d & 1) for d in range(devices)]
    parts = [mine, lax.ppermute(mine, AXES, [(d, d ^ (1 if o else 16)) for d, o in enumerate(owner)])]
    bit = 32
    while bit < devices:
        mine = parts[0] + parts[1]
        parts = [mine, swapped(mine, bit)]
        bit *= 2
    coefs = lax.all_to_all(solve_leaf(parts, devices), AXES, 0, 0, tiled=True)
    tree, fresh = row_outputs(table, x, coefs)
    return grad.reshape(-1), tree.reshape(-1), fresh.reshape(-1)


def solution(mesh):
    rows = P(AXES)
    return jax.shard_map(
        body,
        mesh=mesh,
        in_specs=(P(AXES, None), rows, rows, rows, rows, rows),
        out_specs=(rows, rows, rows),
        check_vma=False,
    )
```

```python
import functools

import jax
import jax.numpy as jnp
import numpy as np
from jax import lax
from jax.experimental import pallas as pl
from jax.experimental.pallas import tpu as pltpu
from jax.sharding import PartitionSpec as P

LEAVES = 16
MAXQ = 128
LAMBDA = 1.0
SHRINKAGE = 0.1
AXES = ("doc", "leaf")
LANE = 128
EXTRA = 8
STRIP = 32
GROUP = 16
NEAR = ((0, 4, 2, 1), (7, 6, 5, 3))
PART = 4
VMEM_LIMIT = 32 * 1024 * 1024
F32 = jnp.float32
BF16 = jnp.bfloat16


def iota(shape, dim):
    return lax.broadcasted_iota(jnp.int32, shape, dim)


def lanes_of(block_rows):
    return jnp.concatenate(
        [block_rows[b : b + 1, :] for b in range(block_rows.shape[0])], axis=1
    )


def position():
    return lax.axis_index("doc") * lax.axis_size("leaf") + lax.axis_index("leaf")


def slot_mask(me):
    return (me & 1) * 8 + ((me >> 2) & 3) * 2 + ((me >> 1) & 1)


def other_core(codes):
    return tuple(code + LEAVES // 2 for code in codes)


def fetch(sources, places, sems):
    copies = [
        pltpu.make_async_copy(src, dst, sems.at[n])
        for n, (src, dst) in enumerate(zip(sources, places))
    ]
    for copy in copies:
        copy.start()
    return copies


def edge_kernel(
    query_hbm, label_hbm, rank_hbm, score_hbm, leaf_hbm,
    inner_ref, outer_ref, table_ref, query, label, rank, score, leaf, sems,
):
    odd = (position() & 1) == 1
    copies = fetch(
        (query_hbm, label_hbm, rank_hbm, score_hbm, leaf_hbm),
        (query, label, rank, score, leaf),
        sems,
    )
    blocks = query.shape[0]
    for copy in copies:
        copy.wait()
    for n, ref in enumerate((query, label, rank, score, leaf)):
        value = ref[...].astype(F32)
        table_ref[n] = value
        if n < 4:
            first, last = value[0:1, :], value[blocks - 1 : blocks, :]
            inner_ref[n : n + 1, :] = jnp.where(odd, first, last)
            outer_ref[n : n + 1, :] = jnp.where(odd, last, first)


def edges(query, label, rank, score, leaf):
    blocks = score.shape[0]
    anywhere = pl.BlockSpec(memory_space=pltpu.HBM)
    vmem = pl.BlockSpec(memory_space=pltpu.VMEM)
    edge = jax.ShapeDtypeStruct((4, LANE), F32)
    whole = pltpu.VMEM((blocks, LANE), jnp.int32)
    return pl.pallas_call(
        edge_kernel,
        out_shape=(edge, edge, jax.ShapeDtypeStruct((5, blocks, LANE), F32)),
        in_specs=[anywhere] * 5,
        out_specs=(vmem,) * 3,
        scratch_shapes=[whole, whole, whole, pltpu.VMEM((blocks, LANE), F32), whole]
        + [pltpu.SemaphoreType.DMA((5,))],
    )(query, label, rank, score, leaf)


def pair_tables(query, label, rank, score, rows, cols, packed_cols):
    count = query.shape[0]
    gain = jnp.exp2(label)
    disc = 1.0 / jnp.log2(1.0 + jnp.maximum(rank, 1.0))
    expo = jnp.exp(score)
    for slot, value in enumerate((query, gain, disc, expo)):
        rows[slot, 0:count, :] = value
        turned = value.T
        for b in range(count):
            cols[slot, b * LANE : (b + 1) * LANE, :] = jnp.broadcast_to(
                turned[:, b : b + 1], (LANE, LANE)
            )
    grade = label.T
    turned = (
        jnp.where(grade >= 1.0, 1, 0)
        + jnp.where(grade >= 2.0, 1 << 8, 0)
        + jnp.where(grade >= 3.0, 1 << 16, 0)
        + jnp.where(grade >= 4.0, 1 << 24, 0)
    )
    for b in range(count):
        packed_cols[b * LANE : (b + 1) * LANE, :] = jnp.broadcast_to(
            turned[:, b : b + 1], (LANE, LANE)
        )


def rank_table():
    positions = iota((LANE, LANE), 0).astype(F32) + 1.0
    return positions, 1.0 / jnp.log2(1.0 + positions)


def pair_sums(own, start, tiles, rows, cols, packed_cols):
    own_q = rows[0, pl.ds(own, 1), :]
    own_g = rows[1, pl.ds(own, 1), :]
    own_d = rows[2, pl.ds(own, 1), :]
    own_e = rows[3, pl.ds(own, 1), :]
    grad_sum = jnp.zeros((8, LANE), F32)
    hess_sum = jnp.zeros((8, LANE), F32)
    counts = jnp.zeros((8, LANE), jnp.int32)
    for chunk in range(tiles * LANE // 8):
        at = pl.ds(pl.multiple_of(start * LANE + chunk * 8, 8), 8)
        far_e = cols[3, at, :]
        same = cols[0, at, :] == own_q
        gap = own_g - cols[1, at, :]
        signed = jnp.where(same, gap * jnp.abs(own_d - cols[2, at, :]), 0.0)
        inv = 1.0 / (own_e + far_e)
        scaled = signed * inv
        grad_sum = grad_sum + scaled * jnp.where(gap > 0.0, far_e, own_e)
        hess_sum = hess_sum + jnp.abs(scaled) * (far_e * inv)
        counts = counts + jnp.where(same, packed_cols[at, :], 0)
    return grad_sum, hess_sum, counts


def pair_finish(sums, own_e, ranked):
    positions, position_disc = ranked
    grad_sum, hess_sum, counts = sums
    count = jnp.sum(counts, axis=0, keepdims=True)
    grad = jnp.sum(grad_sum, axis=0, keepdims=True)
    hess = jnp.sum(hess_sum, axis=0, keepdims=True) * own_e
    ideal = jnp.zeros((LANE, LANE), F32)
    for k in range(4):
        count_k = (lax.shift_right_logical(count, 8 * k) & 255).astype(F32)
        ideal = ideal + jnp.where(positions <= count_k, float(1 << k), 0.0)
    ideal = jnp.sum(ideal * position_disc, axis=0, keepdims=True)
    norm = 1.0 / jnp.maximum(ideal, 1.0)
    return -norm * grad, norm * hess


def leaf_sums(x, turned, hess_all, grad_all, leaf_all, weighted, moment_s, hsum_s, total_s):
    n_rows = leaf_all.shape[1]
    weighted[...] = (turned * hess_all).astype(BF16)
    member = leaf_all == iota((LEAVES, n_rows), 0)
    member_low = jnp.where(member, 1.0, 0.0).astype(BF16)
    grad_low = jnp.where(member, grad_all, 0.0).astype(BF16)
    moment_s[...] = jnp.dot(grad_low, x, preferred_element_type=F32)
    hsum_s[...] = lax.dot_general(
        member_low, weighted[...], (((1,), (1,)), ((), ())), preferred_element_type=F32
    )
    htot = jnp.sum(jnp.where(member, hess_all, 0.0), axis=1, keepdims=True)
    gtot = jnp.sum(jnp.where(member, grad_all, 0.0), axis=1, keepdims=True)
    lane_at = iota((LEAVES, LANE), 1)
    total_s[...] = jnp.where(lane_at == 0, htot, jnp.where(lane_at == 1, gtot, 0.0))


def pack_grams(x_ref, leaf_all, weighted, moment_s, hsum_s, total_s, out_ref, codes):
    half = x_ref.shape[1] // 2
    mask = slot_mask(position())
    down = iota((half, half), 0)
    across = iota((half, half), 1)

    for slot, code in enumerate(codes):
        leaf = mask ^ code
        chosen = jnp.where(leaf_all == leaf.astype(F32), 1.0, 0.0).astype(BF16)
        gram = jnp.dot(weighted[...] * chosen, x_ref[...], preferred_element_type=F32)
        out_ref[slot, 0:half, :] = gram[half:, :half]
        out_ref[slot, half : 2 * half, :] = jnp.where(
            down >= across, gram[:half, :half], gram[half:, half:]
        )
        diagonal = jnp.sum(
            jnp.where(down == across, gram[half:, half:], 0.0), axis=0, keepdims=True
        )
        hs = hsum_s[pl.ds(leaf, 1), :]
        mo = moment_s[pl.ds(leaf, 1), :]
        to = total_s[pl.ds(leaf, 1), :]
        out_ref[slot, 2 * half :, :] = jnp.concatenate(
            [diagonal, hs[:, :half], hs[:, half:], mo[:, :half], mo[:, half:], to]
            + [jnp.zeros((EXTRA - 6, LANE), F32)],
            axis=0,
        )


def interior_kernel(table, grad_ref, hess_ref, part_ref, count_ref, rows, cols, packed_cols):
    blocks = grad_ref.shape[0]
    pair_tables(table[0], table[1], table[2], table[3], rows, cols, packed_cols)
    nothing = jnp.zeros((1, LANE), F32)
    for ref in (grad_ref, hess_ref):
        ref[0:1, :] = nothing
        ref[blocks - 1 : blocks, :] = nothing

    for n, b in enumerate((0, blocks - 1)):
        sums = pair_sums(b, n * (blocks - 2), 2, rows, cols, packed_cols)
        part_ref[2 * n], part_ref[2 * n + 1], count_ref[n] = sums
    ranked = rank_table()

    def one_block(b, carry):
        sums = pair_sums(b, b - 1, 3, rows, cols, packed_cols)
        grad, hess = pair_finish(sums, rows[3, pl.ds(b, 1), :], ranked)
        grad_ref[pl.ds(b, 1), :] = grad
        hess_ref[pl.ds(b, 1), :] = hess
        return carry

    lax.fori_loop(1, blocks - 1, one_block, 0, unroll=6)


def boundary_kernel(
    table, x_ref, inner, outer, grad_part, hess_part, part_ref, count_ref,
    grad_ref, send_ref, weighted, moment_s, hsum_s, total_s, x_out,
    rows, cols, packed_cols,
):
    blocks = grad_ref.shape[0]
    final = blocks - 1
    me = position()
    devices = lax.axis_size("doc") * lax.axis_size("leaf")

    odd = (me & 1) == 1

    def window(slot):
        near = inner[slot : slot + 1, :]
        far = outer[slot : slot + 1, :]
        return jnp.concatenate(
            [
                jnp.where(odd, near, far),
                table[slot, 0:1, :],
                table[slot, final:, :],
                jnp.where(odd, far, near),
            ],
            axis=0,
        )

    ids = window(0)
    at = iota(ids.shape, 0)
    outside = ((at == 0) & (me == 0)) | ((at == 3) & (me == devices - 1))
    pair_tables(
        jnp.where(outside, -1.0, ids), window(1), window(2), window(3), rows, cols, packed_cols
    )
    ranked = rank_table()
    ends = []
    for n in range(2):
        sums = pair_sums(n + 1, 3 * n, 1, rows, cols, packed_cols)
        held = (part_ref[2 * n], part_ref[2 * n + 1], count_ref[n])
        sums = [a + b for a, b in zip(sums, held)]
        ends.append(pair_finish(sums, rows[3, n + 1 : n + 2, :], ranked))
    (head_grad, head_hess), (tail_grad, tail_hess) = ends
    grads = jnp.concatenate([head_grad, grad_part[1:final, :], tail_grad], axis=0)
    hesses = jnp.concatenate([head_hess, hess_part[1:final, :], tail_hess], axis=0)
    grad_ref[...] = grads
    x_out[...] = x_ref[...]
    leaf_all = lanes_of(table[4])
    leaf_sums(
        x_ref[...], x_ref[...].astype(F32).T, lanes_of(hesses), lanes_of(grads), leaf_all,
        weighted, moment_s, hsum_s, total_s,
    )
    pack_grams(x_ref, leaf_all, weighted, moment_s, hsum_s, total_s, send_ref, other_core(NEAR[0]))


def gram_kernel(codes, table, x_ref, weighted, moment_s, hsum_s, total_s, out_ref):
    pack_grams(
        x_ref, lanes_of(table[4]), weighted, moment_s, hsum_s, total_s, out_ref, codes
    )


def table_scratch(count):
    return [
        pltpu.VMEM((4, 8 * pl.cdiv(count, 8), LANE), F32),
        pltpu.VMEM((4, count * LANE, LANE), F32),
        pltpu.VMEM((count * LANE, LANE), jnp.int32),
    ]


def on_chip(kernel, outs, scratch, args, cost=None):
    vmem = pl.BlockSpec(memory_space=pltpu.VMEM)
    return pl.pallas_call(
        kernel,
        out_shape=tuple(jax.ShapeDtypeStruct(shape, kind) for shape, kind in outs),
        in_specs=[vmem] * len(args),
        out_specs=(vmem,) * len(outs),
        scratch_shapes=scratch,
        compiler_params=pltpu.CompilerParams(vmem_limit_bytes=VMEM_LIMIT),
        cost_estimate=cost,
    )(*args)


def interior(table):
    _, blocks, _ = table.shape
    cost = pl.CostEstimate(
        flops=20000 * blocks * LANE * LANE, bytes_accessed=blocks * LANE * LANE, transcendentals=0
    )
    row = ((blocks, LANE), F32)
    parts = (((4, 8, LANE), F32), ((2, 8, LANE), jnp.int32))
    return on_chip(interior_kernel, (row, row, *parts), table_scratch(blocks), (table,), cost)


def boundary(table, x, inner, outer, grad, *parts):
    n_rows, feats = x.shape
    outs = (
        (grad.shape, F32),
        ((PART, feats + EXTRA, LANE), F32),
        ((feats, n_rows), BF16),
        ((LEAVES, feats), F32),
        ((LEAVES, feats), F32),
        ((LEAVES, LANE), F32),
        (x.shape, x.dtype),
    )
    return on_chip(
        boundary_kernel, outs, table_scratch(4), (table, x, inner, outer, grad, *parts)
    )


def gram_part(codes, table, x, weighted, moment, hsum, totals):
    n_rows, feats = x.shape
    cost = pl.CostEstimate(
        flops=8 * PART * n_rows * feats * feats, bytes_accessed=n_rows * feats, transcendentals=0
    )
    outs = (((PART, feats + EXTRA, LANE), F32),)
    kernel = functools.partial(gram_kernel, codes)
    return on_chip(kernel, outs, [], (table, x, weighted, moment, hsum, totals), cost)[0]


def fold_kernel(keep_ref, other_ref, *outs):
    for n, out in enumerate(outs):
        out[...] = keep_ref[n] + other_ref[n]


def fold(keep, other):
    return on_chip(fold_kernel, ((keep.shape[1:], F32),) * keep.shape[0], [], (keep, other))


def tree_sum(values):
    while len(values) > 1:
        values = [a + b for a, b in zip(values[::2], values[1::2])]
    return values[0]


def total_kernel(*refs):
    refs[-1][...] = tree_sum([ref[...] for ref in refs[:-1]])


def total(parts):
    return on_chip(total_kernel, ((parts[0].shape, F32),), [], parts)[0]


def eliminate(tiles, at, offset):
    size = tiles[at].shape[0]
    down = iota((size, LANE), 0)
    scale = jnp.ones((size, LANE), F32)
    for base in range(0, size, GROUP):
        first = offset + base
        columns = [
            jnp.broadcast_to(tiles[at][:, first + j : first + j + 1], (size, LANE))
            for j in range(GROUP)
        ]
        for j in range(GROUP):
            p = base + j
            inverse = 1.0 / columns[j][p : p + 1, :]
            scale = jnp.where(down == p, inverse, scale)
            factor = jnp.where(down == p, 0.0, columns[j]) * inverse
            for k in range(j + 1, GROUP):
                columns[k] = columns[k] - factor * columns[k][p : p + 1, :]
            tiles = [t if t is None else t - factor * t[p : p + 1, :] for t in tiles]
    return [t if t is None else t * scale for t in tiles]


def three(value):
    top = value.astype(BF16)
    left = value - top.astype(F32)
    middle = left.astype(BF16)
    return top, middle, (left - middle.astype(F32)).astype(BF16)


def left_parts(value):
    top, middle, bottom = three(value)
    return jnp.concatenate([top, top, middle, top, middle, bottom], axis=1)


def right_parts(value):
    top, middle, bottom = three(value)
    return jnp.concatenate([top, middle, top, bottom, middle, top], axis=0)


def solve_kernel(*refs):
    ins, out_ref = refs[:-1], refs[-1]
    summed = tree_sum([ref[...] for ref in ins])
    feats = summed.shape[0] - EXTRA
    half = feats // 2
    corner = summed[:half]
    mixed = summed[half:feats]
    extra = [summed[feats + n : feats + n + 1] for n in range(6)]
    turned = mixed.T
    down = iota((half, half), 0)
    across = iota((half, half), 1)
    diag_row, hs0, hs1, mo0, mo1, totals = extra
    upper_left = jnp.where(down >= across, mixed, turned)
    lower_right = jnp.where(down < across, mixed, jnp.where(down > across, turned, diag_row))
    htot = totals[:, 0:1]
    gtot = totals[:, 1:2]
    inv_den = 1.0 / (htot + LAMBDA)
    rhs0 = hs0 * (gtot * inv_den) - mo0
    rhs1 = hs1 * (gtot * inv_den) - mo1
    columns = jnp.concatenate(
        [hs0, hs1, rhs0, rhs1, jnp.zeros((4, LANE), F32)], axis=0
    ).T
    hc0 = columns[:, 0:1] * inv_den
    hc1 = columns[:, 1:2] * inv_den
    eye = jnp.where(down == across, LAMBDA, 0.0)
    top = [
        upper_left + eye - hc0 * hs0,
        corner.T - hc0 * hs1,
        jnp.where(across == 0, columns[:, 2:3], 0.0),
    ]
    low = [
        corner - hc1 * hs0,
        lower_right + eye - hc1 * hs1,
        jnp.where(across == 0, columns[:, 3:4], 0.0),
    ]
    per_tile = LANE // STRIP
    count = feats // STRIP
    strips = []
    for s in range(count):
        source = top if s < per_tile else low
        start = (s % per_tile) * STRIP
        strips.append([t[start : start + STRIP] for t in source])
    for s in range(count):
        tile, offset = s // per_tile, (s % per_tile) * STRIP
        done = eliminate([None] * tile + strips[s][tile:], tile, offset)
        strips[s] = done
        solved = right_parts(jnp.concatenate(done[tile:], axis=1))
        later = [s + 1] if s + 1 < count else []
        others = [i for i in range(count) if i not in (s, s + 1)]
        for group in (later, others):
            if not group:
                continue
            left = jnp.concatenate(
                [strips[i][tile][:, offset : offset + STRIP] for i in group], axis=0
            )
            change = jnp.dot(left_parts(left), solved, preferred_element_type=F32)
            for q, i in enumerate(group):
                part = change[q * STRIP : (q + 1) * STRIP]
                strips[i] = [
                    t if n < tile else t - part[:, (n - tile) * LANE : (n - tile + 1) * LANE]
                    for n, t in enumerate(strips[i])
                ]
    right = [strips[s][2] for s in range(count)]
    w0 = jnp.concatenate(right[:per_tile], axis=0).T[0:1, :]
    w1 = jnp.concatenate(right[per_tile:], axis=0).T[0:1, :]
    dotted = jnp.sum(hs0 * w0 + hs1 * w1, axis=1, keepdims=True)
    intercept = -(gtot + dotted) * inv_den
    result = jnp.concatenate(
        [w0, w1, jnp.broadcast_to(intercept, (1, LANE)), jnp.zeros((1, LANE), F32)], axis=0
    )
    out_ref[...] = jnp.broadcast_to(result[None], out_ref.shape)


def solve_leaf(parts, copies):
    return on_chip(solve_kernel, (((copies, 4, LANE), F32),), [], parts)[0]


def output_kernel(table, x_ref, coef_ref, tree_ref, new_ref):
    slots = [coef_ref[(n >> 3) * 17 + (n & 7) * 2] for n in range(LEAVES)]
    low = jnp.concatenate([c[0:1, :] for c in slots], axis=0)
    high = jnp.concatenate([c[1:2, :] for c in slots], axis=0)
    shift = jnp.concatenate([c[2:3, :] for c in slots], axis=0)[:, 0:1]
    coefs = jnp.concatenate([low, high], axis=1)
    stacked = jnp.concatenate(three(coefs), axis=0)
    parts = lax.dot_general(
        stacked, x_ref[...], (((1,), (1,)), ((), ())), preferred_element_type=F32
    )
    per_leaf = (
        parts[:LEAVES] + (parts[LEAVES : 2 * LEAVES] + parts[2 * LEAVES :])
    ) + shift
    leaf_all = lanes_of(table[4])
    leaf_at = iota(per_leaf.shape, 0).astype(F32)
    chosen = jnp.sum(jnp.where(leaf_all == leaf_at, per_leaf, 0.0), axis=0, keepdims=True)
    for b in range(tree_ref.shape[0]):
        piece = chosen[:, b * LANE : (b + 1) * LANE]
        tree_ref[b : b + 1, :] = piece
        new_ref[b : b + 1, :] = table[3, b : b + 1, :] + SHRINKAGE * piece


def row_outputs(table, x, coefs):
    row = (table.shape[1:], F32)
    return on_chip(output_kernel, (row, row), [], (table, x, coefs))


def body(features, scores, labels, query_ids, ranks, leaf_ids):
    devices = lax.axis_size("doc") * lax.axis_size("leaf")
    n_rows = features.shape[0]
    score, label, query, rank, leaf = [
        v.reshape(n_rows // LANE, LANE) for v in (scores, labels, query_ids, ranks, leaf_ids)
    ]

    def swapped(value, flip):
        return lax.ppermute(value, AXES, [(i, i ^ flip) for i in range(devices)])

    x = features
    inner, outer, table = edges(query, label, rank, score, leaf)
    inner = swapped(inner, 1)
    outer = lax.ppermute(
        outer, AXES, [(i, (i + (1 if i % 2 else -1)) % devices) for i in range(devices)]
    )
    grad, *rest = interior(table)
    grad, send, *sums, held = boundary(table, x, inner, outer, grad, *rest)
    chunks = []
    for codes in NEAR:
        if chunks:
            send = gram_part(other_core(codes), table, held, *sums)
        other = swapped(send, 1)
        folded = fold(gram_part(codes, table, held, *sums), other)
        chunks += [swapped(c, 2 * code) if code else c for c, code in zip(folded, codes)]
    mine = total(chunks)
    owner = [(d >> 4 & 1) == (d & 1) for d in range(devices)]
    parts = [mine, lax.ppermute(mine, AXES, [(d, d ^ (1 if o else 16)) for d, o in enumerate(owner)])]
    bit = 32
    while bit < devices:
        mine = parts[0] + parts[1]
        parts = [mine, swapped(mine, bit)]
        bit *= 2
    coefs = lax.all_to_all(solve_leaf(parts, devices), AXES, 0, 0, tiled=True)
    tree, fresh = row_outputs(table, x, coefs)
    return grad.reshape(-1), tree.reshape(-1), fresh.reshape(-1)


def solution(mesh):
    rows = P(AXES)
    return jax.shard_map(
        body,
        mesh=mesh,
        in_specs=(P(AXES, None), rows, rows, rows, rows, rows),
        out_specs=(rows, rows, rows),
        check_vma=False,
    )
```
